32 devices in a mesh: groups: 2 (over y), gx: 8 (over z, x), gy: 2 (over core).
Axes of the slice: x: 2, y: 2, z: 4, core: 2. Of those that a mesh axis runs over, the one named last changes fastest.
Arguments:
- displacement: float32 [3, 16, 64, 128], P(None, ('groups', 'gx'), 'gy'), parts along dimension 1, may hold values from -6 to 6
- velocity: float32 [3, 16, 64, 128], P(None, ('groups', 'gx'), 'gy'), parts along dimension 1, may hold values from -6 to 6
- species: int32 [8, 64, 128], P('gx', 'gy'), may hold values from 0 to 1, as said below
- mass_factor: float32 [8, 64, 128], P('gx', 'gy'), may hold values from 0.6 to 1.6
- spring: float32 [8, 64, 128], P('gx', 'gy'), may hold values from 0.5 to 2
- force_blocks: float32 [8, 3, 3], replicated, may hold values from -0.6 to 0.6
- shell_table: int32 [3, 9], replicated, may hold values from 0 to 7
Outputs:
- mass_grad: float32 [16, 64, 128], P(('groups', 'gx'), 'gy'), parts along dimension 0
- spring_grad: float32 [16, 64, 128], P(('groups', 'gx'), 'gy'), parts along dimension 0
The draws below stay inside these ranges and needn't reach their ends.
There are 2 independent parts, one for each index of `groups`. The reference program is written for one: setup_inputs(seed, part) draws one part's arguments, and reference() takes and returns one part's arrays. A program takes and returns all parts, laid end to end along the dimension named above; an argument that names none is the same for every part. Nothing has to cross between parts.
Inputs may be any that keep to these rules, and one draw needn't show every extreme that they name: `species`: 1 marks germanium, 0 silicon; the lower half of the transport dimension is mostly silicon, the upper half mostly germanium.
All inputs are finite; a program needn't handle non-finite values.
Results may differ from the reference program's by a relative error of at most 0.0003.
Values sent between devices are 32-bit elements; how exact they have to be, the bound alone decides.
No kernel may reach another device: no remote copies, remote signals or barrier semaphores. Data moves between devices by JAX's collectives and lax.ppermute only.
A program may use at most 128 MiB of HBM per device.

```python
import math
import jax
import jax.numpy as jnp
from jax import lax

ZCELLS = 128
STEPS = 5
BLOCKS = 8
NX = 8
NY = 64


def draw_species(key, part):
    key = jax.random.fold_in(key, 11)
    depth_index = lax.broadcasted_iota(jnp.int32, (NX, NY, ZCELLS), 2)
    upper = (depth_index >= ZCELLS // 2).astype(jnp.int32)
    flipped = (jax.random.randint(key, (NX, NY, ZCELLS), 0, 20) < 3).astype(jnp.int32)
    return (upper + flipped - 2 * upper * flipped).astype(jnp.int32)


def touch_ends(values, stream_key, low, largest):
    dims = values.shape
    index_at = [jax.random.randint(jax.random.fold_in(stream_key, axis), (), 0, dims[axis]) for axis in range(len(dims))]
    values = values.at[tuple(index_at)].set(low)
    longest = dims.index(max(dims))
    index_at[longest] = (index_at[longest] + 1) % dims[longest]
    return values.at[tuple(index_at)].set(largest)


def level_of(own_key, extent, split, low, top_value):
    factor_of, own = 1.0, jax.random.fold_in(own_key, 6)
    for axis_at, blocks in split:
        draws = jnp.exp(jax.random.uniform(jax.random.fold_in(own, axis_at), (blocks,), jnp.float32, low / len(split), top_value / len(split)))
        factor_of = factor_of * jnp.repeat(draws, extent[axis_at] // blocks).reshape([-1 if axis == axis_at else 1 for axis in range(len(extent))])
    return factor_of


def noise(own_key, extent, spread, bound, split=(), held_as=jnp.bfloat16):
    result = spread * jax.random.normal(own_key, extent, jnp.float32)
    if split:
        result = result * level_of(own_key, extent, split, -0.22, 0.18)
    return jnp.clip(result, -bound, bound).astype(held_as)


def setup_inputs(seed: int = 0, part: int = 0) -> dict:
    streams_of = jax.random.split(jax.random.key(seed), 8)
    part_keys = jax.random.split(jax.random.fold_in(streams_of[7], part), 8)
    displacement = noise(part_keys[0], (3, NX, NY, ZCELLS), 1.0, 6.0, ((1, 8), (2, 2)), jnp.float32)
    velocity = noise(part_keys[1], (3, NX, NY, ZCELLS), 1.0, 6.0, ((1, 8), (2, 2)), jnp.float32)
    species = draw_species(jax.random.fold_in(streams_of[7], 71), part)
    mass_factor = jnp.clip(jnp.exp(math.log(1.6) - 0.98082923 * jax.random.uniform(streams_of[3], (NX, NY, ZCELLS), jnp.float32) ** level_of(streams_of[3], (NX, NY, ZCELLS), ((0, 8), (1, 2)), -0.2, 0.2)), 0.6, 1.6)
    spring = jnp.clip(jnp.exp(math.log(2.0) - 1.3862944 * jax.random.uniform(streams_of[4], (NX, NY, ZCELLS), jnp.float32) ** level_of(streams_of[4], (NX, NY, ZCELLS), ((0, 8), (1, 2)), -0.2, 0.2)), 0.5, 2.0)
    force_blocks = noise(streams_of[5], (BLOCKS, 3, 3), 0.15, 0.6, (), jnp.float32)
    shell_table = touch_ends(jax.random.randint(streams_of[6], (3, 9), 0, BLOCKS), jax.random.fold_in(streams_of[6], 1), 0, BLOCKS - 1).astype(jnp.int32)
    return dict(displacement=displacement, velocity=velocity, species=species, mass_factor=mass_factor, spring=spring, force_blocks=force_blocks, shell_table=shell_table)


DIRECTIONS = ((1, 0, 0), (0, 1, 0), (0, 0, 1), (1, 1, 0), (1, -1, 0), (1, 0, 1), (1, 0, -1), (0, 1, 1), (0, 1, -1))
time_step = 0.5
germanium_ratio = 1.5856


def shift_depth(field, depth):
    if depth == 0:
        return field
    border = jnp.zeros_like(field[..., :1])
    if depth > 0:
        return jnp.concatenate([field[..., 1:], border], axis=-1)
    return jnp.concatenate([border, field[..., :-1]], axis=-1)


def neighbour(field, offset):
    rolled = jnp.roll(field, (-offset[0], -offset[1]), axis=(-3, -2))
    return shift_depth(rolled, offset[2])


def pair_blocks(force_blocks, shell_table):
    symmetric = 0.5 * (force_blocks + jnp.swapaxes(force_blocks, 1, 2))
    labels = jnp.arange(force_blocks.shape[0], dtype=jnp.int32)
    selector = (shell_table[:, :, None] == labels[None, None, :]).astype(jnp.float32)
    return jnp.einsum("kdn,nrc->kdrc", selector, symmetric, precision=lax.Precision.HIGHEST)


def coupling(kinds, centre_kind, other_kind, valid):
    weight_low = (1.0 - centre_kind) * (1.0 - other_kind)
    weight_high = centre_kind * other_kind
    weight_mixed = 1.0 - weight_low - weight_high
    return [[(weight_low * kinds[0, first, second] + weight_mixed * kinds[1, first, second]
              + weight_high * kinds[2, first, second]) * valid for second in range(3)] for first in range(3)]


def apply_coupling(matrix, difference):
    return jnp.stack([matrix[first][0] * difference[0] + matrix[first][1] * difference[1]
                      + matrix[first][2] * difference[2] for first in range(3)])


def operator_terms(value, value_at, partner, partner_at, species_float, spring, params_at, valid_at, blocks):
    total = jnp.zeros_like(value)
    spring_part = jnp.zeros_like(spring)
    for direction in range(9):
        for flipped in (1, -1):
            offset = tuple(flipped * entry for entry in DIRECTIONS[direction])
            other_kind, other_spring = params_at(offset)
            matrix = coupling(blocks[:, direction], species_float, other_kind, valid_at(offset))
            image = apply_coupling(matrix, value - value_at(offset))
            total = total + 0.5 * (spring + other_spring) * image
            if partner is not None:
                spring_part = spring_part + 0.5 * jnp.sum((partner - partner_at(offset)) * image, axis=0)
    return total, spring_part


def reference(displacement, velocity, species, mass_factor, spring, force_blocks, shell_table):
    blocks = pair_blocks(force_blocks, shell_table)
    species_float = species.astype(jnp.float32)
    species_mass = 1.0 + germanium_ratio * species_float
    mass = species_mass * mass_factor
    filled = jnp.ones_like(spring)

    def params_at(offset):
        return neighbour(species_float, offset), neighbour(spring, offset)

    def valid_at(offset):
        return neighbour(filled, offset)

    def acting(value, partner):
        value_at = lambda offset: neighbour(value, offset)
        partner_at = None if partner is None else (lambda offset: neighbour(partner, offset))
        return operator_terms(value, value_at, partner, partner_at, species_float, spring, params_at, valid_at, blocks)

    half_step = 0.5 * time_step
    drift = 0.5 * time_step * time_step
    states = [displacement]
    accels = [-acting(displacement, None)[0] / mass]
    moving = velocity
    for count in range(STEPS):
        advanced = states[-1] + time_step * moving + drift * accels[-1]
        fresh = -acting(advanced, None)[0] / mass
        moving = moving + half_step * (accels[-1] + fresh)
        states.append(advanced)
        accels.append(fresh)
    depth_index = lax.broadcasted_iota(jnp.int32, spring.shape, 2)
    detect = (depth_index >= ZCELLS // 2).astype(jnp.float32)
    velocity_bar = detect * mass * moving
    mass_bar = 0.5 * detect * jnp.sum(moving * moving, axis=0)
    spring_bar = jnp.zeros_like(spring)
    state_bar = jnp.zeros_like(displacement)
    accel_bar = jnp.zeros_like(displacement)
    for level in range(STEPS, -1, -1):
        if level > 0:
            accel_bar = accel_bar + half_step * velocity_bar
        scaled = accel_bar / mass
        pushed, spring_term = acting(scaled, states[level])
        state_bar = state_bar - pushed
        mass_bar = mass_bar - jnp.sum(accel_bar * accels[level], axis=0) / mass
        spring_bar = spring_bar - spring_term
        if level > 0:
            accel_bar = drift * state_bar + half_step * velocity_bar
            velocity_bar = velocity_bar + time_step * state_bar
    return mass_bar * species_mass, spring_bar
```

```python
import jax
import jax.numpy as jnp
from jax import lax
from jax.experimental import pallas as pl
from jax.experimental.pallas import tpu as pltpu
from jax.sharding import PartitionSpec as P

ZCELLS = 128
STEPS = 5
TILE = 8

DIRECTIONS = (
    (1, 0, 0),
    (0, 1, 0),
    (0, 0, 1),
    (1, 1, 0),
    (1, -1, 0),
    (1, 0, 1),
    (1, 0, -1),
    (0, 1, 1),
    (0, 1, -1),
)
PAIRS = ((0, 0), (0, 1), (0, 2), (1, 1), (1, 2), (2, 2))
ENTRY = ((0, 1, 2), (1, 3, 4), (2, 4, 5))
time_step = 0.5
germanium_ratio = 1.5856
half_step = 0.5 * time_step
LEVELS = 2 * (STEPS + 1)
FIELDS = 9


def kernel(ring, half, *refs):
    blocks_in = refs[: 2 * ring]
    force_ref, table_ref, mass_grad, spring_grad = refs[2 * ring : 2 * ring + 4]
    fields, speed, accel, kind, stiff, inverse, coef, own_sum, carry, up_sum, down_sum, ray, ray_up, ray_down = refs[
        2 * ring + 4 :
    ]
    rows = 2 * half
    tiles = rows // TILE
    me = lax.axis_index("gx")
    depth_index = lax.broadcasted_iota(jnp.int32, (TILE, ZCELLS), 1)

    def ahead(value):
        return pltpu.roll(value, ZCELLS - 1, 1)

    def behind(value):
        return pltpu.roll(value, 1, 1)

    def along(value, depth):
        return ahead(value) if depth > 0 else behind(value) if depth < 0 else value

    def wrap(slab):
        return lax.rem(slab, ring)

    def at(tile, shift=0):
        return pl.ds(TILE + TILE * tile + shift, TILE)

    def plain(tile):
        return pl.ds(TILE * tile, TILE)

    def put_ringed(ref, where, tile, value):
        ref[where + (at(tile),)] = value
        if tile == 0:
            ref[where + (at(tiles),)] = value
        if tile == tiles - 1:
            ref[where + (at(-1),)] = value

    for message in range(ring):
        slab = lax.bitwise_xor(me, message)
        for side in range(2):
            source = blocks_in[2 * message + side]
            for tile in range(half // TILE):
                target = side * (half // TILE) + tile
                for comp in range(3):
                    put_ringed(fields, (0, slab, comp), target, source[comp, plain(tile)])
                    speed[slab, comp, plain(target)] = source[3 + comp, plain(tile)]
                sort = source[6, plain(tile)]
                put_ringed(kind, (slab,), target, sort)
                put_ringed(stiff, (slab,), target, source[8, plain(tile)])
                mass = (1.0 + germanium_ratio * sort) * source[7, plain(tile)]
                inverse[slab, plain(target)] = -1.0 / mass

    def block_entries(direction):
        result = []
        for pair in range(3):
            index = table_ref[pair, direction]
            result.append(
                [0.5 * (force_ref[index, a, b] + force_ref[index, b, a]) for a, b in PAIRS]
            )
        return result

    def valid(depth):
        if depth > 0:
            return depth_index < ZCELLS - 1
        return depth_index > 0

    def matrix(entries, total_kind):
        low = total_kind < 0.5
        mixed = total_kind < 1.5
        return [
            jnp.where(low, entries[0][n], jnp.where(mixed, entries[1][n], entries[2][n]))
            for n in range(6)
        ]

    for direction, (dx, dy, dz) in enumerate(DIRECTIONS):
        entries = block_entries(direction)

        def fill(slab, _, direction=direction, dx=dx, dy=dy, dz=dz, entries=entries):
            other = wrap(slab + dx)
            for tile in range(tiles):
                total_kind = kind[slab, at(tile)] + along(kind[other, at(tile, dy)], dz)
                bond = 0.5 * (stiff[slab, at(tile)] + along(stiff[other, at(tile, dy)], dz))
                if dz != 0:
                    bond = jnp.where(valid(dz), bond, 0.0)
                for n, entry in enumerate(matrix(entries, total_kind)):
                    coef[slab, 6 * direction + n, plain(tile)] = bond * entry
            return 0

        lax.fori_loop(0, ring, fill, 0)

    def push(slab, direction, tile, difference):
        entry = [coef[slab, 6 * direction + n, plain(tile)] for n in range(6)]
        return [
            entry[ENTRY[a][0]] * difference[0]
            + entry[ENTRY[a][1]] * difference[1]
            + entry[ENTRY[a][2]] * difference[2]
            for a in range(3)
        ]

    def sub(first, second):
        return [a - b for a, b in zip(first, second)]

    def add(first, second):
        return [a + b for a, b in zip(first, second)]

    def load(level, slab, tile, shift=0):
        return [fields[level, slab, comp, at(tile, shift)] for comp in range(3)]

    def turned(values, depth):
        return [along(value, depth) for value in values]

    def cross_bonds(level, slab, tile, centre):
        beside = wrap(slab + 1)
        straight = load(level, beside, tile)
        first = push(slab, 0, tile, sub(centre, straight))
        third = push(slab, 5, tile, sub(centre, turned(straight, 1)))
        fourth = push(slab, 6, tile, sub(centre, turned(straight, -1)))
        upper = push(slab, 3, tile, sub(centre, load(level, beside, tile, 1)))
        lower = push(slab, 4, tile, sub(centre, load(level, beside, tile, -1)))
        here = add(add(add(first, third), fourth), add(upper, lower))
        there = add(first, add(turned(third, -1), turned(fourth, 1)))
        return here, there, upper, lower

    def step(level, _):
        reach = LEVELS - 1 - level
        count = jnp.minimum(ring, 2 * reach + 1)
        low = wrap(me - lax.div(count, 2) + 2 * ring)
        middle = level == STEPS
        kick = jnp.where((level == 0) | (level == STEPS) | (level == STEPS + 1), half_step, time_step)
        keep = jnp.where(middle, 0.0, 1.0)
        detect = jnp.where(depth_index >= ZCELLS // 2, 1.0, 0.0)
        drift = jnp.where(middle, detect, jnp.full((TILE, ZCELLS), time_step))

        before = wrap(low + ring - 1)
        for tile in range(tiles):
            centre = load(level, before, tile)
            _, there, upper, lower = cross_bonds(level, before, tile, centre)
            for comp in range(3):
                carry[0, comp, plain(tile)] = there[comp]
                carry[1, comp, plain(tile)] = upper[comp]
                put_ringed(down_sum, (1, comp), tile, lower[comp])

        def one(number, _):
            slab = wrap(low + number)
            slot = lax.rem(number, 2)
            for tile in range(tiles):
                centre = load(level, slab, tile)
                here, there, upper, lower = cross_bonds(level, slab, tile, centre)
                beyond = load(level, slab, tile, 1)
                second = push(slab, 1, tile, sub(centre, beyond))
                seventh = push(slab, 7, tile, sub(centre, turned(beyond, 1)))
                eighth = push(slab, 8, tile, sub(centre, turned(beyond, -1)))
                deep = push(slab, 2, tile, sub(centre, turned(centre, 1)))
                here = add(add(here, deep), add(second, add(seventh, eighth)))
                here = sub(here, turned(deep, -1))
                lift = add(second, add(turned(seventh, -1), turned(eighth, 1)))
                for comp in range(3):
                    own_sum[comp, plain(tile)] = here[comp] - carry[0, comp, plain(tile)]
                    carry[0, comp, plain(tile)] = there[comp]
                    put_ringed(up_sum, (comp,), tile, lift[comp] + carry[1, comp, plain(tile)])
                    carry[1, comp, plain(tile)] = upper[comp]
                    put_ringed(down_sum, (slot, comp), tile, lower[comp])
            mine = jnp.where(slab == me, 1, 0)
            for tile in range(tiles):
                over = inverse[slab, plain(tile)]
                for comp in range(3):
                    total = (
                        own_sum[comp, plain(tile)]
                        - up_sum[comp, at(tile, -1)]
                        - down_sum[1 - slot, comp, at(tile, 1)]
                    )
                    change = total * over
                    accel[level, mine, comp, plain(tile)] = change
                    moved = speed[slab, comp, plain(tile)] + kick * change
                    speed[slab, comp, plain(tile)] = keep * moved
                    fresh = keep * fields[level, slab, comp, at(tile)] + drift * moved
                    put_ringed(fields, (level + 1, slab, comp), tile, fresh)
            return 0

        lax.fori_loop(0, count, one, 0)
        return 0

    lax.fori_loop(0, LEVELS - 1, step, 0)

    weights = [half_step if level in (0, STEPS) else time_step for level in range(STEPS + 1)]
    own_tiles = half // TILE
    for tile in range(own_tiles):
        last = [fields[STEPS + 1, me, comp, at(tile)] for comp in range(3)]
        bar = 0.5 * (last[0] * last[0] + last[1] * last[1] + last[2] * last[2])
        for level in range(STEPS + 1):
            dual = [fields[LEVELS - 1 - level, me, comp, at(tile)] for comp in range(3)]
            moves = [accel[level, 1, comp, plain(tile)] for comp in range(3)]
            bar = bar - weights[level] * (
                dual[0] * moves[0] + dual[1] * moves[1] + dual[2] * moves[2]
            )
        mass_grad[plain(tile)] = bar * (1.0 + germanium_ratio * kind[me, at(tile)])

    entries_of = [block_entries(direction) for direction in range(9)]

    def strain(slab, direction, tile):
        dx, dy, dz = DIRECTIONS[direction]
        other = wrap(slab + dx)
        total_kind = kind[slab, at_dynamic(tile)] + along(kind[other, at_dynamic(tile, dy)], dz)
        entry = matrix(entries_of[direction], total_kind)
        result = None
        for level in range(STEPS + 1):
            parts = []
            for where in (level, LEVELS - 1 - level):
                parts.append(
                    [
                        fields[where, slab, comp, at_dynamic(tile)]
                        - along(fields[where, other, comp, at_dynamic(tile, dy)], dz)
                        for comp in range(3)
                    ]
                )
            state, dual = parts
            image = [
                entry[ENTRY[a][0]] * dual[0] + entry[ENTRY[a][1]] * dual[1] + entry[ENTRY[a][2]] * dual[2]
                for a in range(3)
            ]
            term = weights[level] * (state[0] * image[0] + state[1] * image[1] + state[2] * image[2])
            result = term if result is None else result + term
        if dz != 0:
            result = jnp.where(valid(dz), result, 0.0)
        return result

    def at_dynamic(tile, shift=0):
        return pl.ds(TILE + TILE * tile + shift, TILE)

    past = wrap(me + ring - 1)

    def rays(tile, _):
        total = strain(me, 2, tile)
        total = total + behind(total)
        for direction in (0, 3, 4, 5, 6):
            total = total + strain(me, direction, tile)
        second, seventh, eighth = (strain(me, direction, tile) for direction in (1, 7, 8))
        total = total + (second + (seventh + eighth))
        lift = second + (behind(seventh) + ahead(eighth)) + strain(past, 3, tile)
        total = total + strain(past, 0, tile)
        total = total + behind(strain(past, 5, tile)) + ahead(strain(past, 6, tile))
        ray[at_dynamic(tile)] = total
        ray_up[at_dynamic(tile)] = lift
        ray_down[at_dynamic(tile)] = strain(past, 4, tile)
        return 0

    lax.fori_loop(0, own_tiles, rays, 0)
    final = tiles - 1
    ray_up[at(-1)] = (
        strain(me, 1, final)
        + (behind(strain(me, 7, final)) + ahead(strain(me, 8, final)))
        + strain(past, 3, final)
    )
    ray_down[at(own_tiles)] = strain(past, 4, own_tiles)
    for tile in range(own_tiles):
        spring_grad[plain(tile)] = -0.5 * (
            ray[at(tile)] + ray_up[at(tile, -1)] + ray_down[at(tile, 1)]
        )


def gathered_body(displacement, velocity, species, mass_factor, spring, force_blocks, shell_table):
    ring = lax.axis_size("gx")
    half = spring.shape[1]
    rows = 2 * half
    own = jnp.concatenate(
        [displacement[:, 0], velocity[:, 0], species.astype(jnp.float32), mass_factor, spring]
    )

    def swap_slabs(value, mask):
        return lax.ppermute(value, "gx", [(i, i ^ mask) for i in range(ring)])

    def swap_halves(value):
        return lax.ppermute(value, "gy", [(0, 1), (1, 0)])

    messages = {0: own, 1: swap_slabs(own, 1)}
    for mask in range(2, ring, 2):
        messages[mask] = swap_slabs(own, mask)
        messages[mask + 1] = swap_slabs(messages[mask], 1)
    operands = []
    for mask in range(ring):
        operands += [messages[mask], swap_halves(messages[mask])]

    padded = rows + 2 * TILE
    scratch = [
        (LEVELS, ring, 3, padded, ZCELLS),
        (ring, 3, rows, ZCELLS),
        (LEVELS, 2, 3, rows, ZCELLS),
        (ring, padded, ZCELLS),
        (ring, padded, ZCELLS),
        (ring, rows, ZCELLS),
        (ring, 54, rows, ZCELLS),
        (3, rows, ZCELLS),
        (2, 3, rows, ZCELLS),
        (3, padded, ZCELLS),
        (2, 3, padded, ZCELLS),
        (padded, ZCELLS),
        (padded, ZCELLS),
        (padded, ZCELLS),
    ]
    mass_grad, spring_grad = pl.pallas_call(
        lambda *refs: kernel(ring, half, *refs),
        out_shape=[jax.ShapeDtypeStruct((half, ZCELLS), jnp.float32)] * 2,
        in_specs=[pl.BlockSpec(memory_space=pltpu.VMEM)] * (2 * ring)
        + [pl.BlockSpec(memory_space=pltpu.SMEM)] * 2,
        out_specs=[pl.BlockSpec(memory_space=pltpu.VMEM)] * 2,
        scratch_shapes=[pltpu.VMEM(shape, jnp.float32) for shape in scratch],
        compiler_params=pltpu.CompilerParams(vmem_limit_bytes=56 * 1024 * 1024),
    )(*operands, force_blocks, shell_table)
    return mass_grad[None], spring_grad[None]


def padded_2(cells, sides, width):
    for axis, dim in sides:
        count = lax.axis_size(axis)
        head = lax.slice_in_dim(cells, 0, width, axis=dim)
        tail = lax.slice_in_dim(cells, cells.shape[dim] - width, cells.shape[dim], axis=dim)
        cells = jnp.concatenate(
            [
                lax.ppermute(tail, axis, [(i, (i + 1) % count) for i in range(count)]),
                cells,
                lax.ppermute(head, axis, [((i + 1) % count, i) for i in range(count)]),
            ],
            axis=dim,
        )
    return cells


def shift_depth(field, depth):
    if depth == 0:
        return field
    border = jnp.zeros_like(field[..., :1])
    if depth > 0:
        return jnp.concatenate([field[..., 1:], border], axis=-1)
    return jnp.concatenate([border, field[..., :-1]], axis=-1)


def pair_blocks(force_blocks, shell_table):
    symmetric = 0.5 * (force_blocks + jnp.swapaxes(force_blocks, 1, 2))
    labels = jnp.arange(force_blocks.shape[0], dtype=jnp.int32)
    selector = (shell_table[:, :, None] == labels[None, None, :]).astype(jnp.float32)
    return jnp.einsum("kdn,nrc->kdrc", selector, symmetric, precision=lax.Precision.HIGHEST)


def coupling(kinds, centre_kind, other_kind, valid):
    weight_low = (1.0 - centre_kind) * (1.0 - other_kind)
    weight_high = centre_kind * other_kind
    weight_mixed = 1.0 - weight_low - weight_high
    return [
        [
            (
                weight_low * kinds[0, first, second]
                + weight_mixed * kinds[1, first, second]
                + weight_high * kinds[2, first, second]
            )
            * valid
            for second in range(3)
        ]
        for first in range(3)
    ]


def apply_coupling(matrix, difference):
    return jnp.stack(
        [
            matrix[first][0] * difference[0]
            + matrix[first][1] * difference[1]
            + matrix[first][2] * difference[2]
            for first in range(3)
        ]
    )


def operator_terms(
    value, value_at, partner, partner_at, species_float, spring, params_at, valid_at, blocks
):
    total = jnp.zeros_like(value)
    spring_part = jnp.zeros_like(spring)
    for direction in range(9):
        for flipped in (1, -1):
            offset = tuple((flipped * entry for entry in DIRECTIONS[direction]))
            other_kind, other_spring = params_at(offset)
            matrix = coupling(blocks[:, direction], species_float, other_kind, valid_at(offset))
            image = apply_coupling(matrix, value - value_at(offset))
            total = total + 0.5 * (spring + other_spring) * image
            if partner is not None:
                spring_part = spring_part + 0.5 * jnp.sum(
                    (partner - partner_at(offset)) * image, axis=0
                )
    return (total, spring_part)


def pick(padded, offset):
    width_x = padded.shape[1] - 2
    width_y = padded.shape[2] - 2
    window = padded[
        :, 1 + offset[0] : 1 + offset[0] + width_x, 1 + offset[1] : 1 + offset[1] + width_y, :
    ]
    return shift_depth(window, offset[2])


def centre(padded):
    return padded[:, 1:-1, 1:-1, :]


def pad_state(field):
    return padded_2(field, (("gx", 1), ("gy", 2)), 1)


def exchanged_body(displacement, velocity, species, mass_factor, spring, force_blocks, shell_table):
    blocks = pair_blocks(force_blocks, shell_table)
    species_float = species.astype(jnp.float32)
    species_mass = 1.0 + germanium_ratio * species_float
    mass = species_mass * mass_factor
    material = padded_2(jnp.stack([species_float, spring]), (("gx", 1), ("gy", 2)), 1)
    filled = jnp.ones_like(spring)

    def params_at(offset):
        beside_all = pick(material, offset)
        return (beside_all[0], beside_all[1])

    def valid_at(offset):
        return shift_depth(filled, offset[2])

    def acting(padded_value, padded_partner):
        value_at = lambda offset: pick(padded_value, offset)
        if padded_partner is None:
            return operator_terms(
                centre(padded_value),
                value_at,
                None,
                None,
                species_float,
                spring,
                params_at,
                valid_at,
                blocks,
            )
        partner_at = lambda offset: pick(padded_partner, offset)
        return operator_terms(
            centre(padded_value),
            value_at,
            centre(padded_partner),
            partner_at,
            species_float,
            spring,
            params_at,
            valid_at,
            blocks,
        )

    half_step = 0.5 * time_step
    drift = 0.5 * time_step * time_step
    states = [displacement]
    padded_states = [pad_state(displacement)]
    accels = [-acting(padded_states[0], None)[0] / mass]
    moving = velocity
    for count in range(STEPS):
        advanced = states[-1] + time_step * moving + drift * accels[-1]
        padded_advanced = pad_state(advanced)
        fresh = -acting(padded_advanced, None)[0] / mass
        moving = moving + half_step * (accels[-1] + fresh)
        states.append(advanced)
        padded_states.append(padded_advanced)
        accels.append(fresh)
    depth_index = lax.broadcasted_iota(jnp.int32, spring.shape, 2)
    detect = (depth_index >= ZCELLS // 2).astype(jnp.float32)
    velocity_bar = detect * mass * moving
    mass_bar = 0.5 * detect * jnp.sum(moving * moving, axis=0)
    spring_bar = jnp.zeros_like(spring)
    state_bar = jnp.zeros_like(displacement)
    accel_bar = jnp.zeros_like(displacement)
    for level in range(STEPS, -1, -1):
        if level > 0:
            accel_bar = accel_bar + half_step * velocity_bar
        scaled = accel_bar / mass
        padded_scaled = padded_2(scaled, (("gx", 1), ("gy", 2)), 1)
        padded_partner = padded_states[level]
        pushed, spring_term = acting(padded_scaled, padded_partner)
        state_bar = state_bar - pushed
        mass_bar = mass_bar - jnp.sum(accel_bar * accels[level], axis=0) / mass
        spring_bar = spring_bar - spring_term
        if level > 0:
            accel_bar = drift * state_bar + half_step * velocity_bar
            velocity_bar = velocity_bar + time_step * state_bar
    return (mass_bar * species_mass, spring_bar)


def solution(mesh):
    small = mesh.shape["gx"] == 8 and mesh.shape["gy"] == 2
    return jax.shard_map(
        gathered_body if small else exchanged_body,
        mesh=mesh,
        in_specs=(
            P(None, ("groups", "gx"), "gy", None),
            P(None, ("groups", "gx"), "gy", None),
            P("gx", "gy", None),
            P("gx", "gy", None),
            P("gx", "gy", None),
            P(),
            P(),
        ),
        out_specs=(P(("groups", "gx"), "gy", None), P(("groups", "gx"), "gy", None)),
        check_vma=False,
    )
```

```python
import jax
import jax.numpy as jnp
from jax import lax
from jax.experimental import pallas as pl
from jax.experimental.pallas import tpu as pltpu
from jax.sharding import PartitionSpec as P

ZCELLS = 128
STEPS = 5
TILE = 8

DIRECTIONS = (
    (1, 0, 0),
    (0, 1, 0),
    (0, 0, 1),
    (1, 1, 0),
    (1, -1, 0),
    (1, 0, 1),
    (1, 0, -1),
    (0, 1, 1),
    (0, 1, -1),
)
BONDS = (
    ((0, 0, 0), (1, 0, 0)),
    ((0, 0, 0), (0, 1, 0)),
    ((0, 0, 0), (0, 0, 1)),
    ((0, 0, 0), (1, 1, 0)),
    ((1, 0, 0), (0, 1, 0)),
    ((0, 0, 0), (1, 0, 1)),
    ((1, 0, 0), (0, 0, 1)),
    ((0, 0, 0), (0, 1, 1)),
    ((0, 1, 0), (0, 0, 1)),
)
PAIRS = ((0, 0), (0, 1), (0, 2), (1, 1), (1, 2), (2, 2))
ENTRY = ((0, 1, 2), (1, 3, 4), (2, 4, 5))
time_step = 0.5
germanium_ratio = 1.5856
half_step = 0.5 * time_step
LEVELS = 2 * (STEPS + 1)
FIELDS = 9


def kernel(ring, half, *refs):
    blocks_in = refs[: 2 * ring]
    force_ref, table_ref, mass_grad, spring_grad = refs[2 * ring : 2 * ring + 4]
    (
        fields,
        speed,
        pushes,
        matter,
        inverse,
        coef,
        sums,
        carry,
        ray,
    ) = refs[2 * ring + 4 :]
    rows = 2 * half
    tiles = rows // TILE
    own_tiles = half // TILE
    me = lax.axis_index("gx")
    depth_index = lax.broadcasted_iota(jnp.int32, (TILE, ZCELLS), 1)

    def ahead(value):
        return pltpu.roll(value, ZCELLS - 1, 1)

    def behind(value):
        return pltpu.roll(value, 1, 1)

    def wrap(slab):
        return lax.rem(slab, ring)

    def at(tile, shift=0):
        return pl.ds(TILE * tile + shift, TILE)

    def late(tile, shift=0):
        return pl.ds(TILE + TILE * tile + shift, TILE)

    def put_field(level, slab, comp, tile, value):
        deeper = ahead(value)
        fields[0, level, slab, comp, at(tile)] = value
        fields[1, level, slab, comp, at(tile)] = deeper
        if tile == 0:
            fields[0, level, slab, comp, at(tiles)] = value
            fields[1, level, slab, comp, at(tiles)] = deeper

    for message in range(ring):
        slab = lax.bitwise_xor(me, message)
        for side in range(2):
            source = blocks_in[2 * message + side]
            for tile in range(own_tiles):
                target = side * own_tiles + tile
                for comp in range(3):
                    put_field(0, slab, comp, target, source[comp, at(tile)])
                    speed[slab, comp, at(target)] = time_step * source[3 + comp, at(tile)]
                sort = source[6, at(tile)]
                for which, value in ((0, sort), (1, source[8, at(tile)])):
                    deeper = ahead(value)
                    for place in (target,) if target else (0, tiles):
                        matter[which, 0, slab, at(place)] = value
                        matter[which, 1, slab, at(place)] = deeper
                mass = (1.0 + germanium_ratio * sort) * source[7, at(tile)]
                inverse[slab, at(target)] = (-time_step * time_step) / mass

    def block_entries(direction):
        result = []
        for pair in range(3):
            index = table_ref[pair, direction]
            result.append([0.5 * (force_ref[index, a, b] + force_ref[index, b, a]) for a, b in PAIRS])
        return result

    inside = depth_index < ZCELLS - 1

    def matrix(entries, total_kind):
        low = total_kind < 0.5
        mixed = total_kind < 1.5
        return [
            jnp.where(low, entries[0][n], jnp.where(mixed, entries[1][n], entries[2][n])) for n in range(6)
        ]

    def ends(ref, where, slab, direction, tile):
        return [
            ref[where[0] + (dz,) + where[1] + (wrap(slab + dx),) + where[2] + (at(tile, dy),)]
            for dx, dy, dz in BONDS[direction]
        ]

    def matter_ends(which, slab, direction, tile):
        return ends(matter, ((which,), (), ()), slab, direction, tile)

    for direction in range(9):
        entries = block_entries(direction)

        def fill(slab, _, direction=direction, entries=entries):
            for tile in range(tiles):
                first, second = matter_ends(0, slab, direction, tile)
                spring_first, spring_second = matter_ends(1, slab, direction, tile)
                bond = 0.5 * (spring_first + spring_second)
                if BONDS[direction][1][2]:
                    bond = jnp.where(inside, bond, 0.0)
                for n, entry in enumerate(matrix(entries, first + second)):
                    coef[slab, 6 * direction + n, at(tile)] = bond * entry
            return 0

        lax.fori_loop(0, ring, fill, 0)

    def product(entry, vector):
        return [
            entry[ENTRY[a][0]] * vector[0] + entry[ENTRY[a][1]] * vector[1] + entry[ENTRY[a][2]] * vector[2]
            for a in range(3)
        ]

    def bonds(level, slab, order):
        beside = wrap(slab + 1)
        for tile in order:
            loaded = {}

            def site(place):
                if place not in loaded:
                    dx, dy, dz = place
                    loaded[place] = [
                        fields[dz, level, beside if dx else slab, comp, at(tile, dy)] for comp in range(3)
                    ]
                return loaded[place]

            def force(direction):
                first, second = BONDS[direction]
                entry = [coef[slab, 6 * direction + n, at(tile)] for n in range(6)]
                return product(entry, [a - b for a, b in zip(site(first), site(second))])

            here, up, deep, across, lift, dive = (None,) * 6

            def add(total, values):
                return values if total is None else [a + b for a, b in zip(total, values)]

            def less(total, values):
                return [-b for b in values] if total is None else [a - b for a, b in zip(total, values)]

            f = force(0)
            here, across = f, f
            f = force(4)
            across, up = [a - b for a, b in zip(across, f)], f
            f = force(6)
            across, deep = [a - b for a, b in zip(across, f)], f
            f = force(1)
            here, up = add(here, f), add(up, f)
            f = force(2)
            here, deep = add(here, f), add(deep, f)
            f = force(8)
            up, deep = [a - b for a, b in zip(up, f)], add(deep, f)
            lift = force(3)
            here = add(here, lift)
            dive = force(5)
            here = add(here, dive)
            both = force(7)
            here = add(here, both)
            for comp in range(3):
                sums[0, slab, comp, late(tile)] = here[comp]
                sums[1, slab, comp, late(tile)] = up[comp]
                sums[2, slab, comp, late(tile)] = deep[comp]
                sums[3, slab, comp, late(tile)] = both[comp]
                carry[0, beside, comp, late(tile)] = across[comp]
                carry[1, beside, comp, late(tile)] = lift[comp]
                carry[2, beside, comp, late(tile)] = dive[comp]
                if tile == tiles - 1:
                    sums[1, slab, comp, late(-1)] = up[comp]
                    sums[3, slab, comp, late(-1)] = both[comp]
                    carry[1, beside, comp, late(-1)] = lift[comp]

    def update(level, slab, order, kick, kind):
        mine = jnp.where(slab == me, 1, 0)
        detect = depth_index >= ZCELLS // 2
        for tile in order:
            over = kick * inverse[slab, at(tile)]
            for comp in range(3):
                deep = sums[2, slab, comp, late(tile)] + carry[2, slab, comp, late(tile)]
                deep = deep + sums[3, slab, comp, late(tile, -1)]
                total = sums[0, slab, comp, late(tile)] - carry[0, slab, comp, late(tile)]
                total = total - (sums[1, slab, comp, late(tile, -1)] + carry[1, slab, comp, late(tile, -1)])
                change = (total - behind(deep)) * over
                if kind != "dual":
                    pushes[level, mine, comp, at(tile)] = change
                moved = speed[slab, comp, at(tile)] + change
                if kind == "middle":
                    speed[slab, comp, at(tile)] = jnp.zeros_like(moved)
                    fresh = jnp.where(detect, moved, 0.0)
                else:
                    speed[slab, comp, at(tile)] = moved
                    fresh = fields[0, level, slab, comp, at(tile)] + moved
                put_field(level + 1, slab, comp, tile, fresh)

    def step(level, order, kind):
        reach = LEVELS - 1 - level
        count = jnp.minimum(ring, 2 * reach + 1)
        low = wrap(me - jnp.minimum(reach, ring // 2) + ring)
        more = jnp.where(count < ring, 1, 0)
        kick = jnp.where((level == 0) | (level == STEPS) | (level == STEPS + 1), 0.5, 1.0)

        def first(number, _):
            bonds(level, wrap(low - more + number + ring), order)
            return 0

        def second(number, _):
            update(level, wrap(low + number), order, kick, kind)
            return 0

        lax.fori_loop(0, count + more, first, 0)
        lax.fori_loop(0, count, second, 0)

    everything = list(range(tiles))
    near = [tiles - 1] + list(range(own_tiles + 1))
    wide = LEVELS - TILE

    def run(start, stop, order, kind):
        def one(level, _):
            step(level, order, kind)
            return 0

        lax.fori_loop(start, stop, one, 0)

    run(0, wide, everything, "state")
    run(wide, STEPS, near, "state")
    run(STEPS, STEPS + 1, near, "middle")
    run(STEPS + 1, LEVELS - 1, near, "dual")

    weights = [half_step if level in (0, STEPS) else time_step for level in range(STEPS + 1)]
    for tile in range(own_tiles):
        last = [fields[0, STEPS + 1, me, comp, at(tile)] for comp in range(3)]
        bar = 0.5 * (last[0] * last[0] + last[1] * last[1] + last[2] * last[2])
        for level in range(STEPS + 1):
            for comp in range(3):
                dual = fields[0, LEVELS - 1 - level, me, comp, at(tile)]
                bar = bar - dual * pushes[level, 1, comp, at(tile)]
        bar = bar * (1.0 / (time_step * time_step))
        mass_grad[at(tile)] = bar * (1.0 + germanium_ratio * matter[0, 0, me, at(tile)])

    entries_of = [block_entries(direction) for direction in range(9)]

    def strain(slab, direction, tile):
        first, second = matter_ends(0, slab, direction, tile)
        entry = matrix(entries_of[direction], first + second)
        result = None
        for level in range(STEPS + 1):
            parts = []
            for where in (level, LEVELS - 1 - level):
                pairs = [ends(fields, ((), (where,), (comp,)), slab, direction, tile) for comp in range(3)]
                parts.append([a - b for a, b in pairs])
            state, dual = parts
            image = product(entry, dual)
            term = state[0] * image[0] + state[1] * image[1] + state[2] * image[2]
            term = weights[level] / time_step * term
            result = term if result is None else result + term
        if BONDS[direction][1][2]:
            result = jnp.where(inside, result, 0.0)
        return result

    past = wrap(me + ring - 1)

    def lifted(tile):
        up = strain(me, 1, tile) + strain(me, 4, tile) + strain(me, 8, tile) + strain(past, 3, tile)
        return up, strain(me, 7, tile)

    def rays(tile, _):
        second = strain(me, 1, tile)
        both = strain(me, 7, tile)
        third = strain(me, 2, tile)
        here = strain(me, 0, tile) + second + third + strain(me, 3, tile) + strain(me, 5, tile) + both
        here = here + strain(past, 0, tile) + strain(past, 4, tile) + strain(past, 6, tile)
        eighth = strain(me, 8, tile)
        ray[0, late(tile)] = here
        ray[1, late(tile)] = second + strain(me, 4, tile) + eighth + strain(past, 3, tile)
        ray[2, late(tile)] = third + strain(me, 6, tile) + eighth + strain(past, 5, tile)
        ray[3, late(tile)] = both
        return 0

    lax.fori_loop(0, own_tiles, rays, 0)
    ray[1, late(-1)], ray[3, late(-1)] = lifted(tiles - 1)
    for tile in range(own_tiles):
        deep = ray[2, late(tile)] + ray[3, late(tile, -1)]
        spring_grad[at(tile)] = -0.5 * (ray[0, late(tile)] + ray[1, late(tile, -1)] + behind(deep))


def gathered_body(displacement, velocity, species, mass_factor, spring, force_blocks, shell_table):
    ring = lax.axis_size("gx")
    half = spring.shape[1]
    rows = 2 * half
    own = jnp.concatenate(
        [displacement[:, 0], velocity[:, 0], species.astype(jnp.float32), mass_factor, spring]
    )

    def swap_slabs(value, mask):
        return lax.ppermute(value, "gx", [(i, i ^ mask) for i in range(ring)])

    def swap_halves(value):
        return lax.ppermute(value, "gy", [(0, 1), (1, 0)])

    messages = {0: own, 1: swap_slabs(own, 1)}
    for mask in range(2, ring, 2):
        messages[mask] = swap_slabs(own, mask)
        messages[mask + 1] = swap_slabs(messages[mask], 1)
    operands = []
    for mask in range(ring):
        operands += [messages[mask], swap_halves(messages[mask])]

    padded = rows + TILE
    scratch = [
        (2, LEVELS, ring, 3, padded, ZCELLS),
        (ring, 3, rows, ZCELLS),
        (STEPS + 1, 2, 3, rows, ZCELLS),
        (2, 2, ring, padded, ZCELLS),
        (ring, rows, ZCELLS),
        (ring, 54, rows, ZCELLS),
        (4, ring, 3, padded, ZCELLS),
        (3, ring, 3, padded, ZCELLS),
        (4, padded, ZCELLS),
    ]
    mass_grad, spring_grad = pl.pallas_call(
        lambda *refs: kernel(ring, half, *refs),
        out_shape=[jax.ShapeDtypeStruct((half, ZCELLS), jnp.float32)] * 2,
        in_specs=[pl.BlockSpec(memory_space=pltpu.VMEM)] * (2 * ring)
        + [pl.BlockSpec(memory_space=pltpu.SMEM)] * 2,
        out_specs=[pl.BlockSpec(memory_space=pltpu.VMEM)] * 2,
        scratch_shapes=[pltpu.VMEM(shape, jnp.float32) for shape in scratch],
        compiler_params=pltpu.CompilerParams(vmem_limit_bytes=60 * 1024 * 1024),
    )(*operands, force_blocks, shell_table)
    return mass_grad[None], spring_grad[None]


def padded_2(cells, sides, width):
    for axis, dim in sides:
        count = lax.axis_size(axis)
        head = lax.slice_in_dim(cells, 0, width, axis=dim)
        tail = lax.slice_in_dim(cells, cells.shape[dim] - width, cells.shape[dim], axis=dim)
        cells = jnp.concatenate(
            [
                lax.ppermute(tail, axis, [(i, (i + 1) % count) for i in range(count)]),
                cells,
                lax.ppermute(head, axis, [((i + 1) % count, i) for i in range(count)]),
            ],
            axis=dim,
        )
    return cells


def shift_depth(field, depth):
    if depth == 0:
        return field
    border = jnp.zeros_like(field[..., :1])
    if depth > 0:
        return jnp.concatenate([field[..., 1:], border], axis=-1)
    return jnp.concatenate([border, field[..., :-1]], axis=-1)


def pair_blocks(force_blocks, shell_table):
    symmetric = 0.5 * (force_blocks + jnp.swapaxes(force_blocks, 1, 2))
    labels = jnp.arange(force_blocks.shape[0], dtype=jnp.int32)
    selector = (shell_table[:, :, None] == labels[None, None, :]).astype(jnp.float32)
    return jnp.einsum("kdn,nrc->kdrc", selector, symmetric, precision=lax.Precision.HIGHEST)


def coupling(kinds, centre_kind, other_kind, valid):
    weight_low = (1.0 - centre_kind) * (1.0 - other_kind)
    weight_high = centre_kind * other_kind
    weight_mixed = 1.0 - weight_low - weight_high
    return [
        [
            (
                weight_low * kinds[0, first, second]
                + weight_mixed * kinds[1, first, second]
                + weight_high * kinds[2, first, second]
            )
            * valid
            for second in range(3)
        ]
        for first in range(3)
    ]


def apply_coupling(matrix, difference):
    return jnp.stack(
        [
            matrix[first][0] * difference[0]
            + matrix[first][1] * difference[1]
            + matrix[first][2] * difference[2]
            for first in range(3)
        ]
    )


def operator_terms(
    value, value_at, partner, partner_at, species_float, spring, params_at, valid_at, blocks
):
    total = jnp.zeros_like(value)
    spring_part = jnp.zeros_like(spring)
    for direction in range(9):
        for flipped in (1, -1):
            offset = tuple((flipped * entry for entry in DIRECTIONS[direction]))
            other_kind, other_spring = params_at(offset)
            matrix = coupling(blocks[:, direction], species_float, other_kind, valid_at(offset))
            image = apply_coupling(matrix, value - value_at(offset))
            total = total + 0.5 * (spring + other_spring) * image
            if partner is not None:
                spring_part = spring_part + 0.5 * jnp.sum(
                    (partner - partner_at(offset)) * image, axis=0
                )
    return (total, spring_part)


def pick(padded, offset):
    width_x = padded.shape[1] - 2
    width_y = padded.shape[2] - 2
    window = padded[
        :, 1 + offset[0] : 1 + offset[0] + width_x, 1 + offset[1] : 1 + offset[1] + width_y, :
    ]
    return shift_depth(window, offset[2])


def centre(padded):
    return padded[:, 1:-1, 1:-1, :]


def pad_state(field):
    return padded_2(field, (("gx", 1), ("gy", 2)), 1)


def exchanged_body(displacement, velocity, species, mass_factor, spring, force_blocks, shell_table):
    blocks = pair_blocks(force_blocks, shell_table)
    species_float = species.astype(jnp.float32)
    species_mass = 1.0 + germanium_ratio * species_float
    mass = species_mass * mass_factor
    material = padded_2(jnp.stack([species_float, spring]), (("gx", 1), ("gy", 2)), 1)
    filled = jnp.ones_like(spring)

    def params_at(offset):
        beside_all = pick(material, offset)
        return (beside_all[0], beside_all[1])

    def valid_at(offset):
        return shift_depth(filled, offset[2])

    def acting(padded_value, padded_partner):
        value_at = lambda offset: pick(padded_value, offset)
        if padded_partner is None:
            return operator_terms(
                centre(padded_value),
                value_at,
                None,
                None,
                species_float,
                spring,
                params_at,
                valid_at,
                blocks,
            )
        partner_at = lambda offset: pick(padded_partner, offset)
        return operator_terms(
            centre(padded_value),
            value_at,
            centre(padded_partner),
            partner_at,
            species_float,
            spring,
            params_at,
            valid_at,
            blocks,
        )

    half_step = 0.5 * time_step
    drift = 0.5 * time_step * time_step
    states = [displacement]
    padded_states = [pad_state(displacement)]
    accels = [-acting(padded_states[0], None)[0] / mass]
    moving = velocity
    for count in range(STEPS):
        advanced = states[-1] + time_step * moving + drift * accels[-1]
        padded_advanced = pad_state(advanced)
        fresh = -acting(padded_advanced, None)[0] / mass
        moving = moving + half_step * (accels[-1] + fresh)
        states.append(advanced)
        padded_states.append(padded_advanced)
        accels.append(fresh)
    depth_index = lax.broadcasted_iota(jnp.int32, spring.shape, 2)
    detect = (depth_index >= ZCELLS // 2).astype(jnp.float32)
    velocity_bar = detect * mass * moving
    mass_bar = 0.5 * detect * jnp.sum(moving * moving, axis=0)
    spring_bar = jnp.zeros_like(spring)
    state_bar = jnp.zeros_like(displacement)
    accel_bar = jnp.zeros_like(displacement)
    for level in range(STEPS, -1, -1):
        if level > 0:
            accel_bar = accel_bar + half_step * velocity_bar
        scaled = accel_bar / mass
        padded_scaled = padded_2(scaled, (("gx", 1), ("gy", 2)), 1)
        padded_partner = padded_states[level]
        pushed, spring_term = acting(padded_scaled, padded_partner)
        state_bar = state_bar - pushed
        mass_bar = mass_bar - jnp.sum(accel_bar * accels[level], axis=0) / mass
        spring_bar = spring_bar - spring_term
        if level > 0:
            accel_bar = drift * state_bar + half_step * velocity_bar
            velocity_bar = velocity_bar + time_step * state_bar
    return (mass_bar * species_mass, spring_bar)


def solution(mesh):
    small = mesh.shape["gx"] == 8 and mesh.shape["gy"] == 2
    return jax.shard_map(
        gathered_body if small else exchanged_body,
        mesh=mesh,
        in_specs=(
            P(None, ("groups", "gx"), "gy", None),
            P(None, ("groups", "gx"), "gy", None),
            P("gx", "gy", None),
            P("gx", "gy", None),
            P("gx", "gy", None),
            P(),
            P(),
        ),
        out_specs=(P(("groups", "gx"), "gy", None), P(("groups", "gx"), "gy", None)),
        check_vma=False,
    )
```

```python
import jax
import jax.numpy as jnp
from jax import lax
from jax.experimental import pallas as pl
from jax.experimental.pallas import tpu as pltpu
from jax.sharding import PartitionSpec as P

ZCELLS = 128
STEPS = 5
TILE = 8

DIRECTIONS = (
    (1, 0, 0),
    (0, 1, 0),
    (0, 0, 1),
    (1, 1, 0),
    (1, -1, 0),
    (1, 0, 1),
    (1, 0, -1),
    (0, 1, 1),
    (0, 1, -1),
)
BONDS = (
    ((0, 0, 0), (1, 0, 0)),
    ((0, 0, 0), (0, 1, 0)),
    ((0, 0, 0), (0, 0, 1)),
    ((0, 0, 0), (1, 1, 0)),
    ((1, 0, 0), (0, 1, 0)),
    ((0, 0, 0), (1, 0, 1)),
    ((1, 0, 0), (0, 0, 1)),
    ((0, 0, 0), (0, 1, 1)),
    ((0, 1, 0), (0, 0, 1)),
)
PAIRS = ((0, 0), (0, 1), (0, 2), (1, 1), (1, 2), (2, 2))
ENTRY = ((0, 1, 2), (1, 3, 4), (2, 4, 5))
time_step = 0.5
germanium_ratio = 1.5856
half_step = 0.5 * time_step
LEVELS = 2 * (STEPS + 1)
FIELDS = 9


def kernel(ring, half, *refs):
    blocks_in = refs[: 2 * ring]
    force_ref, table_ref, mass_grad, spring_grad = refs[2 * ring : 2 * ring + 4]
    (
        even_fields,
        odd_fields,
        speed,
        pushes,
        matter,
        inverse,
        coef,
        sums,
        carry,
        ray,
    ) = refs[2 * ring + 4 :]
    rows = 2 * half
    tiles = rows // TILE
    own_tiles = half // TILE
    me = lax.axis_index("gx")
    depth_index = lax.broadcasted_iota(jnp.int32, (TILE, ZCELLS), 1)

    def ahead(value):
        return pltpu.roll(value, ZCELLS - 1, 1)

    def behind(value):
        return pltpu.roll(value, 1, 1)

    def wrap(slab):
        return lax.rem(slab, ring)

    def at(tile, shift=0):
        return pl.ds(TILE * tile + shift, TILE)

    def late(tile, shift=0):
        return pl.ds(TILE + TILE * tile + shift, TILE)

    fields = (even_fields, odd_fields)

    def put_field(odd, number, slab, comp, tile, value):
        deeper = ahead(value)
        for place in (tile,) if tile else (0, tiles):
            fields[odd][0, number, slab, comp, at(place)] = value
            fields[odd][1, number, slab, comp, at(place)] = deeper

    for message in range(ring):
        slab = lax.bitwise_xor(me, message)
        for side in range(2):
            source = blocks_in[2 * message + side]
            for tile in range(own_tiles):
                target = side * own_tiles + tile
                for comp in range(3):
                    put_field(0, 0, slab, comp, target, source[comp, at(tile)])
                    rate = time_step * source[3 + comp, at(tile)]
                    speed[0, slab, comp, at(target)] = rate
                    speed[1, slab, comp, at(target)] = ahead(rate)
                sort = source[6, at(tile)]
                for which, value in ((0, sort), (1, source[8, at(tile)])):
                    deeper = ahead(value)
                    for place in (target,) if target else (0, tiles):
                        matter[which, 0, slab, at(place)] = value
                        matter[which, 1, slab, at(place)] = deeper
                mass = (1.0 + germanium_ratio * sort) * source[7, at(tile)]
                over_mass = (-time_step * time_step) / mass
                inverse[0, slab, at(target)] = over_mass
                inverse[1, slab, at(target)] = ahead(over_mass)

    def block_entries(direction):
        result = []
        for pair in range(3):
            index = table_ref[pair, direction]
            result.append([0.5 * (force_ref[index, a, b] + force_ref[index, b, a]) for a, b in PAIRS])
        return result

    inside = depth_index < ZCELLS - 1

    def matrix(entries, total_kind):
        low = total_kind < 0.5
        mixed = total_kind < 1.5
        return [
            jnp.where(low, entries[0][n], jnp.where(mixed, entries[1][n], entries[2][n])) for n in range(6)
        ]

    def ends(ref, where, slab, direction, tile):
        return [
            ref[where[0] + (dz,) + where[1] + (wrap(slab + dx),) + where[2] + (at(tile, dy),)]
            for dx, dy, dz in BONDS[direction]
        ]

    def matter_ends(which, slab, direction, tile):
        return ends(matter, ((which,), (), ()), slab, direction, tile)

    for direction in range(9):
        entries = block_entries(direction)

        def fill(pair, _, direction=direction, entries=entries):
            for slab, tile in [(2 * pair + which, tile) for which in range(2) for tile in range(tiles)]:
                first, second = matter_ends(0, slab, direction, tile)
                spring_first, spring_second = matter_ends(1, slab, direction, tile)
                bond = 0.5 * (spring_first + spring_second)
                if BONDS[direction][1][2]:
                    bond = jnp.where(inside, bond, 0.0)
                for n, entry in enumerate(matrix(entries, first + second)):
                    coef[slab, 6 * direction + n, at(tile)] = bond * entry
            return 0

        lax.fori_loop(0, ring // 2, fill, 0)

    def product(entry, vector):
        return [
            entry[ENTRY[a][0]] * vector[0] + entry[ENTRY[a][1]] * vector[1] + entry[ENTRY[a][2]] * vector[2]
            for a in range(3)
        ]

    def bonds(odd, number, slab, order):
        beside = wrap(slab + 1)
        for tile in order:
            loaded = {}

            def site(place):
                if place not in loaded:
                    dx, dy, dz = place
                    loaded[place] = [
                        fields[odd][dz, number, beside if dx else slab, comp, at(tile, dy)] for comp in range(3)
                    ]
                return loaded[place]

            def force(direction):
                first, second = BONDS[direction]
                entry = [coef[slab, 6 * direction + n, at(tile)] for n in range(6)]
                return product(entry, [a - b for a, b in zip(site(first), site(second))])

            here, up, deep, across, lift, dive = (None,) * 6

            def add(total, values):
                return values if total is None else [a + b for a, b in zip(total, values)]

            def less(total, values):
                return [-b for b in values] if total is None else [a - b for a, b in zip(total, values)]

            f = force(0)
            here, across = f, f
            f = force(4)
            across, up = [a - b for a, b in zip(across, f)], f
            f = force(6)
            across, deep = [a - b for a, b in zip(across, f)], f
            f = force(1)
            here, up = add(here, f), add(up, f)
            f = force(2)
            here, deep = add(here, f), add(deep, f)
            f = force(8)
            up, deep = [a - b for a, b in zip(up, f)], add(deep, f)
            lift = force(3)
            here = add(here, lift)
            dive = force(5)
            here = add(here, dive)
            both = force(7)
            here = add(here, both)
            for comp in range(3):
                sums[0, slab, comp, late(tile)] = here[comp]
                sums[1, slab, comp, late(tile)] = up[comp]
                sums[2, slab, comp, late(tile)] = deep[comp]
                sums[3, slab, comp, late(tile)] = both[comp]
                carry[0, beside, comp, late(tile)] = across[comp]
                carry[1, beside, comp, late(tile)] = lift[comp]
                carry[2, beside, comp, late(tile)] = dive[comp]
                if tile == tiles - 1:
                    sums[1, slab, comp, late(-1)] = up[comp]
                    sums[3, slab, comp, late(-1)] = both[comp]
                    carry[1, beside, comp, late(-1)] = lift[comp]

    def update(odd, number, slab, order, kick, kind):
        mine = jnp.where(slab == me, 1, 0)
        detect = depth_index >= ZCELLS // 2
        detect = (detect, (depth_index >= ZCELLS // 2 - 1) & inside)
        for tile in order:
            over = [kick * inverse[frame, slab, at(tile)] for frame in range(2)]
            for comp in range(3):
                deep = sums[2, slab, comp, late(tile)] + carry[2, slab, comp, late(tile)]
                deep = deep + sums[3, slab, comp, late(tile, -1)]
                total = sums[0, slab, comp, late(tile)] - carry[0, slab, comp, late(tile)]
                total = total - (sums[1, slab, comp, late(tile, -1)] + carry[1, slab, comp, late(tile, -1)])
                for frame, force in enumerate((total - behind(deep), ahead(total) - deep)):
                    change = force * over[frame]
                    if kind != "dual" and frame == 0:
                        pushes[2 * number + odd, mine, comp, at(tile)] = change
                    moved = speed[frame, slab, comp, at(tile)] + change
                    if kind == "middle":
                        speed[frame, slab, comp, at(tile)] = jnp.zeros_like(moved)
                        fresh = jnp.where(detect[frame], moved, 0.0)
                    else:
                        speed[frame, slab, comp, at(tile)] = moved
                        fresh = fields[odd][frame, number, slab, comp, at(tile)] + moved
                    for place in (tile,) if tile else (0, tiles):
                        fields[1 - odd][frame, number + odd, slab, comp, at(place)] = fresh

    def step(odd, number, order, kind):
        level = 2 * number + odd
        reach = LEVELS - 1 - level
        count = jnp.minimum(ring, 2 * reach + 2)
        low = wrap(me - jnp.minimum(reach + 1, ring // 2) + ring)
        kick = jnp.where((level == 0) | (level == STEPS) | (level == STEPS + 1), 0.5, 1.0)

        def start(place, _):
            bonds(odd, number, wrap(low + place), order)
            return 0

        def both(place, _):
            for tile in order:
                update(odd, number, wrap(low + place + 1), [tile], kick, kind)
                bonds(odd, number, wrap(low + place + 2), [tile])
            return 0

        lax.fori_loop(0, 2, start, 0)
        lax.fori_loop(0, count - 2, both, 0)
        update(odd, number, wrap(low + count - 1), order, kick, kind)
        update(odd, number, low, order, kick, kind)

    everything = list(range(tiles))
    near = [tiles - 1] + list(range(own_tiles + 1))
    wide = LEVELS - TILE

    def run(start, stop, order, kind):
        level = start
        if level % 2:
            step(1, level // 2, order, kind)
            level += 1
        pairs = (stop - level) // 2

        def two(number, _):
            step(0, number, order, kind)
            step(1, number, order, kind)
            return 0

        if pairs:
            lax.fori_loop(level // 2, level // 2 + pairs, two, 0)
        if (stop - level) % 2:
            step(0, stop // 2, order, kind)

    run(0, wide, everything, "state")
    run(wide, STEPS, near, "state")
    run(STEPS, STEPS + 1, near, "middle")
    run(STEPS + 1, LEVELS - 1, near, "dual")

    weights = [half_step if level in (0, STEPS) else time_step for level in range(STEPS + 1)]
    for tile in range(own_tiles):
        last = [fields[(STEPS + 1) % 2][0, (STEPS + 1) // 2, me, comp, at(tile)] for comp in range(3)]
        bar = 0.5 * (last[0] * last[0] + last[1] * last[1] + last[2] * last[2])
        for level in range(STEPS + 1):
            for comp in range(3):
                dual = fields[(LEVELS - 1 - level) % 2][0, (LEVELS - 1 - level) // 2, me, comp, at(tile)]
                bar = bar - dual * pushes[level, 1, comp, at(tile)]
        bar = bar * (1.0 / (time_step * time_step))
        mass_grad[at(tile)] = bar * (1.0 + germanium_ratio * matter[0, 0, me, at(tile)])

    entries_of = [block_entries(direction) for direction in range(9)]

    def strain(slab, direction, tile):
        first, second = matter_ends(0, slab, direction, tile)
        entry = matrix(entries_of[direction], first + second)
        result = None
        for level in range(STEPS + 1):
            parts = []
            for where in (level, LEVELS - 1 - level):
                pairs = [
                    ends(fields[where % 2], ((), (where // 2,), (comp,)), slab, direction, tile)
                    for comp in range(3)
                ]
                parts.append([a - b for a, b in pairs])
            state, dual = parts
            image = product(entry, dual)
            term = state[0] * image[0] + state[1] * image[1] + state[2] * image[2]
            term = weights[level] / time_step * term
            result = term if result is None else result + term
        if BONDS[direction][1][2]:
            result = jnp.where(inside, result, 0.0)
        return result

    past = wrap(me + ring - 1)

    def lifted(tile):
        up = strain(me, 1, tile) + strain(me, 4, tile) + strain(me, 8, tile) + strain(past, 3, tile)
        return up, strain(me, 7, tile)

    def rays(tile, _):
        second = strain(me, 1, tile)
        both = strain(me, 7, tile)
        third = strain(me, 2, tile)
        here = strain(me, 0, tile) + second + third + strain(me, 3, tile) + strain(me, 5, tile) + both
        here = here + strain(past, 0, tile) + strain(past, 4, tile) + strain(past, 6, tile)
        eighth = strain(me, 8, tile)
        ray[0, late(tile)] = here
        ray[1, late(tile)] = second + strain(me, 4, tile) + eighth + strain(past, 3, tile)
        ray[2, late(tile)] = third + strain(me, 6, tile) + eighth + strain(past, 5, tile)
        ray[3, late(tile)] = both
        return 0

    lax.fori_loop(0, own_tiles, rays, 0)
    ray[1, late(-1)], ray[3, late(-1)] = lifted(tiles - 1)
    for tile in range(own_tiles):
        deep = ray[2, late(tile)] + ray[3, late(tile, -1)]
        spring_grad[at(tile)] = -0.5 * (ray[0, late(tile)] + ray[1, late(tile, -1)] + behind(deep))


def pack(displacement, velocity, species, mass_factor, spring, packed):
    for comp in range(3):
        packed[comp] = displacement[comp, 0]
        packed[3 + comp] = velocity[comp, 0]
    packed[6] = species[0].astype(jnp.float32)
    packed[7] = mass_factor[0]
    packed[8] = spring[0]


def gathered_body(displacement, velocity, species, mass_factor, spring, force_blocks, shell_table):
    ring = lax.axis_size("gx")
    half = spring.shape[1]
    rows = 2 * half
    own = pl.pallas_call(
        pack,
        out_shape=jax.ShapeDtypeStruct((FIELDS, half, ZCELLS), jnp.float32),
        in_specs=[pl.BlockSpec(memory_space=pltpu.VMEM)] * 5,
        out_specs=pl.BlockSpec(memory_space=pltpu.VMEM),
    )(displacement, velocity, species, mass_factor, spring)

    def swap_slabs(value, mask):
        return lax.ppermute(value, "gx", [(i, i ^ mask) for i in range(ring)])

    def swap_halves(value):
        return lax.ppermute(value, "gy", [(0, 1), (1, 0)])

    messages = {0: own, 1: swap_slabs(own, 1)}
    for mask in range(2, ring, 2):
        messages[mask] = swap_slabs(own, mask)
        messages[mask + 1] = swap_slabs(messages[mask], 1)
    operands = []
    for mask in range(ring):
        operands += [messages[mask], swap_halves(messages[mask])]

    padded = rows + TILE
    scratch = [
        (2, LEVELS // 2, ring, 3, padded, ZCELLS),
        (2, LEVELS // 2, ring, 3, padded, ZCELLS),
        (2, ring, 3, rows, ZCELLS),
        (STEPS + 1, 2, 3, rows, ZCELLS),
        (2, 2, ring, padded, ZCELLS),
        (2, ring, rows, ZCELLS),
        (ring, 54, rows, ZCELLS),
        (4, ring, 3, padded, ZCELLS),
        (3, ring, 3, padded, ZCELLS),
        (4, padded, ZCELLS),
    ]
    mass_grad, spring_grad = pl.pallas_call(
        lambda *refs: kernel(ring, half, *refs),
        out_shape=[jax.ShapeDtypeStruct((half, ZCELLS), jnp.float32)] * 2,
        in_specs=[pl.BlockSpec(memory_space=pltpu.VMEM)] * (2 * ring)
        + [pl.BlockSpec(memory_space=pltpu.SMEM)] * 2,
        out_specs=[pl.BlockSpec(memory_space=pltpu.VMEM)] * 2,
        scratch_shapes=[pltpu.VMEM(shape, jnp.float32) for shape in scratch],
        compiler_params=pltpu.CompilerParams(vmem_limit_bytes=60 * 1024 * 1024),
    )(*operands, force_blocks, shell_table)
    return mass_grad[None], spring_grad[None]


def padded_2(cells, sides, width):
    for axis, dim in sides:
        count = lax.axis_size(axis)
        head = lax.slice_in_dim(cells, 0, width, axis=dim)
        tail = lax.slice_in_dim(cells, cells.shape[dim] - width, cells.shape[dim], axis=dim)
        cells = jnp.concatenate(
            [
                lax.ppermute(tail, axis, [(i, (i + 1) % count) for i in range(count)]),
                cells,
                lax.ppermute(head, axis, [((i + 1) % count, i) for i in range(count)]),
            ],
            axis=dim,
        )
    return cells


def shift_depth(field, depth):
    if depth == 0:
        return field
    border = jnp.zeros_like(field[..., :1])
    if depth > 0:
        return jnp.concatenate([field[..., 1:], border], axis=-1)
    return jnp.concatenate([border, field[..., :-1]], axis=-1)


def pair_blocks(force_blocks, shell_table):
    symmetric = 0.5 * (force_blocks + jnp.swapaxes(force_blocks, 1, 2))
    labels = jnp.arange(force_blocks.shape[0], dtype=jnp.int32)
    selector = (shell_table[:, :, None] == labels[None, None, :]).astype(jnp.float32)
    return jnp.einsum("kdn,nrc->kdrc", selector, symmetric, precision=lax.Precision.HIGHEST)


def coupling(kinds, centre_kind, other_kind, valid):
    weight_low = (1.0 - centre_kind) * (1.0 - other_kind)
    weight_high = centre_kind * other_kind
    weight_mixed = 1.0 - weight_low - weight_high
    return [
        [
            (
                weight_low * kinds[0, first, second]
                + weight_mixed * kinds[1, first, second]
                + weight_high * kinds[2, first, second]
            )
            * valid
            for second in range(3)
        ]
        for first in range(3)
    ]


def apply_coupling(matrix, difference):
    return jnp.stack(
        [
            matrix[first][0] * difference[0]
            + matrix[first][1] * difference[1]
            + matrix[first][2] * difference[2]
            for first in range(3)
        ]
    )


def operator_terms(
    value, value_at, partner, partner_at, species_float, spring, params_at, valid_at, blocks
):
    total = jnp.zeros_like(value)
    spring_part = jnp.zeros_like(spring)
    for direction in range(9):
        for flipped in (1, -1):
            offset = tuple((flipped * entry for entry in DIRECTIONS[direction]))
            other_kind, other_spring = params_at(offset)
            matrix = coupling(blocks[:, direction], species_float, other_kind, valid_at(offset))
            image = apply_coupling(matrix, value - value_at(offset))
            total = total + 0.5 * (spring + other_spring) * image
            if partner is not None:
                spring_part = spring_part + 0.5 * jnp.sum(
                    (partner - partner_at(offset)) * image, axis=0
                )
    return (total, spring_part)


def pick(padded, offset):
    width_x = padded.shape[1] - 2
    width_y = padded.shape[2] - 2
    window = padded[
        :, 1 + offset[0] : 1 + offset[0] + width_x, 1 + offset[1] : 1 + offset[1] + width_y, :
    ]
    return shift_depth(window, offset[2])


def centre(padded):
    return padded[:, 1:-1, 1:-1, :]


def pad_state(field):
    return padded_2(field, (("gx", 1), ("gy", 2)), 1)


def exchanged_body(displacement, velocity, species, mass_factor, spring, force_blocks, shell_table):
    blocks = pair_blocks(force_blocks, shell_table)
    species_float = species.astype(jnp.float32)
    species_mass = 1.0 + germanium_ratio * species_float
    mass = species_mass * mass_factor
    material = padded_2(jnp.stack([species_float, spring]), (("gx", 1), ("gy", 2)), 1)
    filled = jnp.ones_like(spring)

    def params_at(offset):
        beside_all = pick(material, offset)
        return (beside_all[0], beside_all[1])

    def valid_at(offset):
        return shift_depth(filled, offset[2])

    def acting(padded_value, padded_partner):
        value_at = lambda offset: pick(padded_value, offset)
        if padded_partner is None:
            return operator_terms(
                centre(padded_value),
                value_at,
                None,
                None,
                species_float,
                spring,
                params_at,
                valid_at,
                blocks,
            )
        partner_at = lambda offset: pick(padded_partner, offset)
        return operator_terms(
            centre(padded_value),
            value_at,
            centre(padded_partner),
            partner_at,
            species_float,
            spring,
            params_at,
            valid_at,
            blocks,
        )

    half_step = 0.5 * time_step
    drift = 0.5 * time_step * time_step
    states = [displacement]
    padded_states = [pad_state(displacement)]
    accels = [-acting(padded_states[0], None)[0] / mass]
    moving = velocity
    for count in range(STEPS):
        advanced = states[-1] + time_step * moving + drift * accels[-1]
        padded_advanced = pad_state(advanced)
        fresh = -acting(padded_advanced, None)[0] / mass
        moving = moving + half_step * (accels[-1] + fresh)
        states.append(advanced)
        padded_states.append(padded_advanced)
        accels.append(fresh)
    depth_index = lax.broadcasted_iota(jnp.int32, spring.shape, 2)
    detect = (depth_index >= ZCELLS // 2).astype(jnp.float32)
    velocity_bar = detect * mass * moving
    mass_bar = 0.5 * detect * jnp.sum(moving * moving, axis=0)
    spring_bar = jnp.zeros_like(spring)
    state_bar = jnp.zeros_like(displacement)
    accel_bar = jnp.zeros_like(displacement)
    for level in range(STEPS, -1, -1):
        if level > 0:
            accel_bar = accel_bar + half_step * velocity_bar
        scaled = accel_bar / mass
        padded_scaled = padded_2(scaled, (("gx", 1), ("gy", 2)), 1)
        padded_partner = padded_states[level]
        pushed, spring_term = acting(padded_scaled, padded_partner)
        state_bar = state_bar - pushed
        mass_bar = mass_bar - jnp.sum(accel_bar * accels[level], axis=0) / mass
        spring_bar = spring_bar - spring_term
        if level > 0:
            accel_bar = drift * state_bar + half_step * velocity_bar
            velocity_bar = velocity_bar + time_step * state_bar
    return (mass_bar * species_mass, spring_bar)


def solution(mesh):
    small = mesh.shape["gx"] == 8 and mesh.shape["gy"] == 2
    return jax.shard_map(
        gathered_body if small else exchanged_body,
        mesh=mesh,
        in_specs=(
            P(None, ("groups", "gx"), "gy", None),
            P(None, ("groups", "gx"), "gy", None),
            P("gx", "gy", None),
            P("gx", "gy", None),
            P("gx", "gy", None),
            P(),
            P(),
        ),
        out_specs=(P(("groups", "gx"), "gy", None), P(("groups", "gx"), "gy", None)),
        check_vma=False,
    )
```

```python
import jax
import jax.numpy as jnp
from jax import lax
from jax.experimental import pallas as pl
from jax.experimental.pallas import tpu as pltpu
from jax.sharding import PartitionSpec as P

ZCELLS = 128
STEPS = 5
TILE = 8

DIRECTIONS = (
    (1, 0, 0),
    (0, 1, 0),
    (0, 0, 1),
    (1, 1, 0),
    (1, -1, 0),
    (1, 0, 1),
    (1, 0, -1),
    (0, 1, 1),
    (0, 1, -1),
)
BONDS = (
    ((0, 0, 0), (1, 0, 0)),
    ((0, 0, 0), (0, 1, 0)),
    ((0, 0, 0), (0, 0, 1)),
    ((0, 0, 0), (1, 1, 0)),
    ((1, 0, 0), (0, 1, 0)),
    ((0, 0, 0), (1, 0, 1)),
    ((1, 0, 0), (0, 0, 1)),
    ((0, 0, 0), (0, 1, 1)),
    ((0, 1, 0), (0, 0, 1)),
)
PAIRS = ((0, 0), (0, 1), (0, 2), (1, 1), (1, 2), (2, 2))
ENTRY = ((0, 1, 2), (1, 3, 4), (2, 4, 5))
time_step = 0.5
germanium_ratio = 1.5856
half_step = 0.5 * time_step
LEVELS = 2 * (STEPS + 1)
FIELDS = 9
GROUP = 4


def kernel(ring, half, *refs):
    blocks_in = refs[: 2 * ring]
    force_ref, table_ref, mass_grad, spring_grad = refs[2 * ring : 2 * ring + 4]
    (
        even_fields,
        odd_fields,
        speed,
        pushes,
        matter,
        inverse,
        coef,
        even_sums,
        odd_sums,
        even_carry,
        odd_carry,
        ray,
    ) = refs[2 * ring + 4 :]
    rows = 2 * half
    tiles = rows // TILE
    own_tiles = half // TILE
    me = lax.axis_index("gx")
    depth_index = lax.broadcasted_iota(jnp.int32, (TILE, ZCELLS), 1)

    def ahead(value):
        return pltpu.roll(value, ZCELLS - 1, 1)

    def behind(value):
        return pltpu.roll(value, 1, 1)

    def wrap(slab):
        return lax.rem(slab, ring)

    def at(tile, shift=0):
        return pl.ds(TILE * tile + shift, TILE)

    def late(tile, shift=0):
        return pl.ds(TILE + TILE * tile + shift, TILE)

    fields = (even_fields, odd_fields)
    sums_of = (even_sums, odd_sums)
    carry_of = (even_carry, odd_carry)

    def put_field(odd, number, slab, comp, tile, value):
        deeper = ahead(value)
        for place in (tile,) if tile else (0, tiles):
            fields[odd][0, number, slab, comp, at(place)] = value
            fields[odd][1, number, slab, comp, at(place)] = deeper

    for message in range(ring):
        slab = lax.bitwise_xor(me, message)
        for side in range(2):
            source = blocks_in[2 * message + side]
            for tile in range(own_tiles):
                target = side * own_tiles + tile
                for comp in range(3):
                    put_field(0, 0, slab, comp, target, source[comp, at(tile)])
                    rate = time_step * source[3 + comp, at(tile)]
                    speed[0, slab, comp, at(target)] = rate
                    speed[1, slab, comp, at(target)] = ahead(rate)
                sort = source[6, at(tile)]
                for which, value in ((0, sort), (1, source[8, at(tile)])):
                    deeper = ahead(value)
                    for place in (target,) if target else (0, tiles):
                        matter[which, 0, slab, at(place)] = value
                        matter[which, 1, slab, at(place)] = deeper
                mass = (1.0 + germanium_ratio * sort) * source[7, at(tile)]
                over_mass = (-time_step * time_step) / mass
                inverse[0, slab, at(target)] = over_mass
                inverse[1, slab, at(target)] = ahead(over_mass)

    def block_entries(direction):
        result = []
        for pair in range(3):
            index = table_ref[pair, direction]
            result.append([0.5 * (force_ref[index, a, b] + force_ref[index, b, a]) for a, b in PAIRS])
        return result

    inside = depth_index < ZCELLS - 1

    def matrix(entries, total_kind):
        low = total_kind < 0.5
        mixed = total_kind < 1.5
        return [
            jnp.where(low, entries[0][n], jnp.where(mixed, entries[1][n], entries[2][n])) for n in range(6)
        ]

    def ends(ref, where, slab, direction, tile):
        return [
            ref[where[0] + (dz,) + where[1] + (wrap(slab + dx),) + where[2] + (at(tile, dy),)]
            for dx, dy, dz in BONDS[direction]
        ]

    def matter_ends(which, slab, direction, tile):
        return ends(matter, ((which,), (), ()), slab, direction, tile)

    for direction in range(9):
        entries = block_entries(direction)

        def fill(pair, _, direction=direction, entries=entries):
            for slab, tile in [(GROUP * pair + which, tile) for which in range(GROUP) for tile in range(tiles)]:
                first, second = matter_ends(0, slab, direction, tile)
                spring_first, spring_second = matter_ends(1, slab, direction, tile)
                bond = 0.5 * (spring_first + spring_second)
                if BONDS[direction][1][2]:
                    bond = jnp.where(inside, bond, 0.0)
                for n, entry in enumerate(matrix(entries, first + second)):
                    coef[slab, 6 * direction + n, at(tile)] = bond * entry
            return 0

        lax.fori_loop(0, ring // GROUP, fill, 0)

    def product(entry, vector):
        return [
            entry[ENTRY[a][0]] * vector[0] + entry[ENTRY[a][1]] * vector[1] + entry[ENTRY[a][2]] * vector[2]
            for a in range(3)
        ]

    def bonds(odd, number, slab, order):
        beside = wrap(slab + 1)
        sums, carry = sums_of[odd], carry_of[odd]
        for tile in order:
            loaded = {}

            def site(place):
                if place not in loaded:
                    dx, dy, dz = place
                    loaded[place] = [
                        fields[odd][dz, number, beside if dx else slab, comp, at(tile, dy)] for comp in range(3)
                    ]
                return loaded[place]

            def force(direction):
                first, second = BONDS[direction]
                entry = [coef[slab, 6 * direction + n, at(tile)] for n in range(6)]
                return product(entry, [a - b for a, b in zip(site(first), site(second))])

            here, up, deep, across, lift, dive = (None,) * 6

            def add(total, values):
                return values if total is None else [a + b for a, b in zip(total, values)]

            def less(total, values):
                return [-b for b in values] if total is None else [a - b for a, b in zip(total, values)]

            f = force(0)
            here, across = f, f
            f = force(4)
            across, up = [a - b for a, b in zip(across, f)], f
            f = force(6)
            across, deep = [a - b for a, b in zip(across, f)], f
            f = force(1)
            here, up = add(here, f), add(up, f)
            f = force(2)
            here, deep = add(here, f), add(deep, f)
            f = force(8)
            up, deep = [a - b for a, b in zip(up, f)], add(deep, f)
            lift = force(3)
            here = add(here, lift)
            dive = force(5)
            here = add(here, dive)
            both = force(7)
            here = add(here, both)
            for comp in range(3):
                sums[0, slab, comp, late(tile)] = here[comp]
                sums[1, slab, comp, late(tile)] = up[comp]
                sums[2, slab, comp, late(tile)] = deep[comp]
                sums[3, slab, comp, late(tile)] = both[comp]
                carry[0, beside, comp, late(tile)] = across[comp]
                carry[1, beside, comp, late(tile)] = lift[comp]
                carry[2, beside, comp, late(tile)] = dive[comp]
                if tile == tiles - 1:
                    sums[1, slab, comp, late(-1)] = up[comp]
                    sums[3, slab, comp, late(-1)] = both[comp]
                    carry[1, beside, comp, late(-1)] = lift[comp]

    def update(odd, number, slab, order, kick, kind):
        mine = jnp.where(slab == me, 1, 0)
        sums, carry = sums_of[odd], carry_of[odd]
        detect = depth_index >= ZCELLS // 2
        detect = (detect, (depth_index >= ZCELLS // 2 - 1) & inside)
        for tile in order:
            over = [kick * inverse[frame, slab, at(tile)] for frame in range(2)]
            for comp in range(3):
                deep = sums[2, slab, comp, late(tile)] + carry[2, slab, comp, late(tile)]
                deep = deep + sums[3, slab, comp, late(tile, -1)]
                total = sums[0, slab, comp, late(tile)] - carry[0, slab, comp, late(tile)]
                total = total - (sums[1, slab, comp, late(tile, -1)] + carry[1, slab, comp, late(tile, -1)])
                for frame, force in enumerate((total - behind(deep), ahead(total) - deep)):
                    change = force * over[frame]
                    if kind != "dual" and frame == 0:
                        pushes[2 * number + odd, mine, comp, at(tile)] = change
                    moved = speed[frame, slab, comp, at(tile)] + change
                    if kind == "middle":
                        speed[frame, slab, comp, at(tile)] = jnp.zeros_like(moved)
                        fresh = jnp.where(detect[frame], moved, 0.0)
                    else:
                        speed[frame, slab, comp, at(tile)] = moved
                        fresh = fields[odd][frame, number, slab, comp, at(tile)] + moved
                    for place in (tile,) if tile else (0, tiles):
                        fields[1 - odd][frame, number + odd, slab, comp, at(place)] = fresh

    def span(level):
        count = jnp.minimum(ring, 2 * (LEVELS - level))
        low = jnp.where(count < ring, me + level + ring - LEVELS, me + 2 * level + ring // 2)
        return wrap(low + ring), count

    def middle_part(odd, number, order, kind, low, count, kick):
        def both(pair, _):
            for place in (2 * pair, 2 * pair + 1):
                for tile in order:
                    update(odd, number, wrap(low + place + 1), [tile], kick, kind)
                    bonds(odd, number, wrap(low + place + 2), [tile])
            return 0

        lax.fori_loop(0, lax.div(count - 2, 2), both, 0)

    def step(odd, number, order, kind, final=False):
        level = 2 * number + odd
        low, count = span(level)
        kick = jnp.where((level == 0) | (level == STEPS) | (level == STEPS + 1), 0.5, 1.0)
        middle_part(odd, number, order, kind, low, count, kick)
        ahead_low = span(level + 1)[0]
        for place, slab in enumerate((wrap(low + count - 1), low)):
            for tile in order:
                if not final:
                    bonds(1 - odd, number + odd, wrap(ahead_low + place), [tile])
                update(odd, number, slab, [tile], kick, kind)

    everything = list(range(tiles))
    near = [tiles - 1] + list(range(own_tiles + 1))
    wide = LEVELS - TILE

    def run(start, stop, order, kind):
        level = start
        if level % 2:
            step(1, level // 2, order, kind)
            level += 1
        last = stop == LEVELS - 1
        pairs = (stop - level) // 2

        def two(number, _):
            step(0, number, order, kind)
            step(1, number, order, kind)
            return 0

        if pairs:
            lax.fori_loop(level // 2, level // 2 + pairs, two, 0)
        if (stop - level) % 2:
            step(0, stop // 2, order, kind, last)

    for place in range(2):
        bonds(0, 0, wrap(span(0)[0] + place), everything)
    run(0, wide, everything, "state")
    run(wide, STEPS, near, "state")
    run(STEPS, STEPS + 1, near, "middle")
    run(STEPS + 1, LEVELS - 1, near, "dual")

    weights = [half_step if level in (0, STEPS) else time_step for level in range(STEPS + 1)]
    for tile in range(own_tiles):
        last = [fields[(STEPS + 1) % 2][0, (STEPS + 1) // 2, me, comp, at(tile)] for comp in range(3)]
        bar = 0.5 * (last[0] * last[0] + last[1] * last[1] + last[2] * last[2])
        for level in range(STEPS + 1):
            for comp in range(3):
                dual = fields[(LEVELS - 1 - level) % 2][0, (LEVELS - 1 - level) // 2, me, comp, at(tile)]
                bar = bar - dual * pushes[level, 1, comp, at(tile)]
        bar = bar * (1.0 / (time_step * time_step))
        mass_grad[at(tile)] = bar * (1.0 + germanium_ratio * matter[0, 0, me, at(tile)])

    entries_of = [block_entries(direction) for direction in range(9)]

    def strain(slab, direction, tile):
        first, second = matter_ends(0, slab, direction, tile)
        entry = matrix(entries_of[direction], first + second)
        result = None
        for level in range(STEPS + 1):
            parts = []
            for where in (level, LEVELS - 1 - level):
                pairs = [
                    ends(fields[where % 2], ((), (where // 2,), (comp,)), slab, direction, tile)
                    for comp in range(3)
                ]
                parts.append([a - b for a, b in pairs])
            state, dual = parts
            image = product(entry, dual)
            term = state[0] * image[0] + state[1] * image[1] + state[2] * image[2]
            term = weights[level] / time_step * term
            result = term if result is None else result + term
        if BONDS[direction][1][2]:
            result = jnp.where(inside, result, 0.0)
        return result

    past = wrap(me + ring - 1)

    def lifted(tile):
        up = strain(me, 1, tile) + strain(me, 4, tile) + strain(me, 8, tile) + strain(past, 3, tile)
        return up, strain(me, 7, tile)

    def rays(tile, _):
        second = strain(me, 1, tile)
        both = strain(me, 7, tile)
        third = strain(me, 2, tile)
        here = strain(me, 0, tile) + second + third + strain(me, 3, tile) + strain(me, 5, tile) + both
        here = here + strain(past, 0, tile) + strain(past, 4, tile) + strain(past, 6, tile)
        eighth = strain(me, 8, tile)
        ray[0, late(tile)] = here
        ray[1, late(tile)] = second + strain(me, 4, tile) + eighth + strain(past, 3, tile)
        ray[2, late(tile)] = third + strain(me, 6, tile) + eighth + strain(past, 5, tile)
        ray[3, late(tile)] = both
        return 0

    lax.fori_loop(0, own_tiles, rays, 0)
    ray[1, late(-1)], ray[3, late(-1)] = lifted(tiles - 1)
    for tile in range(own_tiles):
        deep = ray[2, late(tile)] + ray[3, late(tile, -1)]
        spring_grad[at(tile)] = -0.5 * (ray[0, late(tile)] + ray[1, late(tile, -1)] + behind(deep))


def pack(displacement, velocity, species, mass_factor, spring, packed):
    for comp in range(3):
        packed[comp] = displacement[comp, 0]
        packed[3 + comp] = velocity[comp, 0]
    packed[6] = species[0].astype(jnp.float32)
    packed[7] = mass_factor[0]
    packed[8] = spring[0]


def gathered_body(displacement, velocity, species, mass_factor, spring, force_blocks, shell_table):
    ring = lax.axis_size("gx")
    half = spring.shape[1]
    rows = 2 * half
    own = pl.pallas_call(
        pack,
        out_shape=jax.ShapeDtypeStruct((FIELDS, half, ZCELLS), jnp.float32),
        in_specs=[pl.BlockSpec(memory_space=pltpu.VMEM)] * 5,
        out_specs=pl.BlockSpec(memory_space=pltpu.VMEM),
    )(displacement, velocity, species, mass_factor, spring)

    def swap_slabs(value, mask):
        return lax.ppermute(value, "gx", [(i, i ^ mask) for i in range(ring)])

    def swap_halves(value):
        return lax.ppermute(value, "gy", [(0, 1), (1, 0)])

    messages = {0: own, 1: swap_slabs(own, 1)}
    for mask in range(2, ring, 2):
        messages[mask] = swap_slabs(own, mask)
        messages[mask + 1] = swap_slabs(messages[mask], 1)
    operands = []
    for mask in range(ring):
        operands += [messages[mask], swap_halves(messages[mask])]

    padded = rows + TILE
    scratch = [
        (2, LEVELS // 2, ring, 3, padded, ZCELLS),
        (2, LEVELS // 2, ring, 3, padded, ZCELLS),
        (2, ring, 3, rows, ZCELLS),
        (STEPS + 1, 2, 3, rows, ZCELLS),
        (2, 2, ring, padded, ZCELLS),
        (2, ring, rows, ZCELLS),
        (ring, 54, rows, ZCELLS),
        (4, ring, 3, padded, ZCELLS),
        (4, ring, 3, padded, ZCELLS),
        (3, ring, 3, padded, ZCELLS),
        (3, ring, 3, padded, ZCELLS),
        (4, padded, ZCELLS),
    ]
    mass_grad, spring_grad = pl.pallas_call(
        lambda *refs: kernel(ring, half, *refs),
        out_shape=[jax.ShapeDtypeStruct((half, ZCELLS), jnp.float32)] * 2,
        in_specs=[pl.BlockSpec(memory_space=pltpu.VMEM)] * (2 * ring)
        + [pl.BlockSpec(memory_space=pltpu.SMEM)] * 2,
        out_specs=[pl.BlockSpec(memory_space=pltpu.VMEM)] * 2,
        scratch_shapes=[pltpu.VMEM(shape, jnp.float32) for shape in scratch],
        compiler_params=pltpu.CompilerParams(vmem_limit_bytes=60 * 1024 * 1024),
    )(*operands, force_blocks, shell_table)
    return mass_grad[None], spring_grad[None]


def padded_2(cells, sides, width):
    for axis, dim in sides:
        count = lax.axis_size(axis)
        head = lax.slice_in_dim(cells, 0, width, axis=dim)
        tail = lax.slice_in_dim(cells, cells.shape[dim] - width, cells.shape[dim], axis=dim)
        cells = jnp.concatenate(
            [
                lax.ppermute(tail, axis, [(i, (i + 1) % count) for i in range(count)]),
                cells,
                lax.ppermute(head, axis, [((i + 1) % count, i) for i in range(count)]),
            ],
            axis=dim,
        )
    return cells


def shift_depth(field, depth):
    if depth == 0:
        return field
    border = jnp.zeros_like(field[..., :1])
    if depth > 0:
        return jnp.concatenate([field[..., 1:], border], axis=-1)
    return jnp.concatenate([border, field[..., :-1]], axis=-1)


def pair_blocks(force_blocks, shell_table):
    symmetric = 0.5 * (force_blocks + jnp.swapaxes(force_blocks, 1, 2))
    labels = jnp.arange(force_blocks.shape[0], dtype=jnp.int32)
    selector = (shell_table[:, :, None] == labels[None, None, :]).astype(jnp.float32)
    return jnp.einsum("kdn,nrc->kdrc", selector, symmetric, precision=lax.Precision.HIGHEST)


def coupling(kinds, centre_kind, other_kind, valid):
    weight_low = (1.0 - centre_kind) * (1.0 - other_kind)
    weight_high = centre_kind * other_kind
    weight_mixed = 1.0 - weight_low - weight_high
    return [
        [
            (
                weight_low * kinds[0, first, second]
                + weight_mixed * kinds[1, first, second]
                + weight_high * kinds[2, first, second]
            )
            * valid
            for second in range(3)
        ]
        for first in range(3)
    ]


def apply_coupling(matrix, difference):
    return jnp.stack(
        [
            matrix[first][0] * difference[0]
            + matrix[first][1] * difference[1]
            + matrix[first][2] * difference[2]
            for first in range(3)
        ]
    )


def operator_terms(
    value, value_at, partner, partner_at, species_float, spring, params_at, valid_at, blocks
):
    total = jnp.zeros_like(value)
    spring_part = jnp.zeros_like(spring)
    for direction in range(9):
        for flipped in (1, -1):
            offset = tuple((flipped * entry for entry in DIRECTIONS[direction]))
            other_kind, other_spring = params_at(offset)
            matrix = coupling(blocks[:, direction], species_float, other_kind, valid_at(offset))
            image = apply_coupling(matrix, value - value_at(offset))
            total = total + 0.5 * (spring + other_spring) * image
            if partner is not None:
                spring_part = spring_part + 0.5 * jnp.sum(
                    (partner - partner_at(offset)) * image, axis=0
                )
    return (total, spring_part)


def pick(padded, offset):
    width_x = padded.shape[1] - 2
    width_y = padded.shape[2] - 2
    window = padded[
        :, 1 + offset[0] : 1 + offset[0] + width_x, 1 + offset[1] : 1 + offset[1] + width_y, :
    ]
    return shift_depth(window, offset[2])


def centre(padded):
    return padded[:, 1:-1, 1:-1, :]


def pad_state(field):
    return padded_2(field, (("gx", 1), ("gy", 2)), 1)


def exchanged_body(displacement, velocity, species, mass_factor, spring, force_blocks, shell_table):
    blocks = pair_blocks(force_blocks, shell_table)
    species_float = species.astype(jnp.float32)
    species_mass = 1.0 + germanium_ratio * species_float
    mass = species_mass * mass_factor
    material = padded_2(jnp.stack([species_float, spring]), (("gx", 1), ("gy", 2)), 1)
    filled = jnp.ones_like(spring)

    def params_at(offset):
        beside_all = pick(material, offset)
        return (beside_all[0], beside_all[1])

    def valid_at(offset):
        return shift_depth(filled, offset[2])

    def acting(padded_value, padded_partner):
        value_at = lambda offset: pick(padded_value, offset)
        if padded_partner is None:
            return operator_terms(
                centre(padded_value),
                value_at,
                None,
                None,
                species_float,
                spring,
                params_at,
                valid_at,
                blocks,
            )
        partner_at = lambda offset: pick(padded_partner, offset)
        return operator_terms(
            centre(padded_value),
            value_at,
            centre(padded_partner),
            partner_at,
            species_float,
            spring,
            params_at,
            valid_at,
            blocks,
        )

    half_step = 0.5 * time_step
    drift = 0.5 * time_step * time_step
    states = [displacement]
    padded_states = [pad_state(displacement)]
    accels = [-acting(padded_states[0], None)[0] / mass]
    moving = velocity
    for count in range(STEPS):
        advanced = states[-1] + time_step * moving + drift * accels[-1]
        padded_advanced = pad_state(advanced)
        fresh = -acting(padded_advanced, None)[0] / mass
        moving = moving + half_step * (accels[-1] + fresh)
        states.append(advanced)
        padded_states.append(padded_advanced)
        accels.append(fresh)
    depth_index = lax.broadcasted_iota(jnp.int32, spring.shape, 2)
    detect = (depth_index >= ZCELLS // 2).astype(jnp.float32)
    velocity_bar = detect * mass * moving
    mass_bar = 0.5 * detect * jnp.sum(moving * moving, axis=0)
    spring_bar = jnp.zeros_like(spring)
    state_bar = jnp.zeros_like(displacement)
    accel_bar = jnp.zeros_like(displacement)
    for level in range(STEPS, -1, -1):
        if level > 0:
            accel_bar = accel_bar + half_step * velocity_bar
        scaled = accel_bar / mass
        padded_scaled = padded_2(scaled, (("gx", 1), ("gy", 2)), 1)
        padded_partner = padded_states[level]
        pushed, spring_term = acting(padded_scaled, padded_partner)
        state_bar = state_bar - pushed
        mass_bar = mass_bar - jnp.sum(accel_bar * accels[level], axis=0) / mass
        spring_bar = spring_bar - spring_term
        if level > 0:
            accel_bar = drift * state_bar + half_step * velocity_bar
            velocity_bar = velocity_bar + time_step * state_bar
    return (mass_bar * species_mass, spring_bar)


def solution(mesh):
    small = mesh.shape["gx"] == 8 and mesh.shape["gy"] == 2
    return jax.shard_map(
        gathered_body if small else exchanged_body,
        mesh=mesh,
        in_specs=(
            P(None, ("groups", "gx"), "gy", None),
            P(None, ("groups", "gx"), "gy", None),
            P("gx", "gy", None),
            P("gx", "gy", None),
            P("gx", "gy", None),
            P(),
            P(),
        ),
        out_specs=(P(("groups", "gx"), "gy", None), P(("groups", "gx"), "gy", None)),
        check_vma=False,
    )
```

```python
import jax
import jax.numpy as jnp
from jax import lax
from jax.experimental import pallas as pl
from jax.experimental.pallas import tpu as pltpu
from jax.sharding import PartitionSpec as P

ZCELLS = 128
STEPS = 5
TILE = 8

DIRECTIONS = (
    (1, 0, 0),
    (0, 1, 0),
    (0, 0, 1),
    (1, 1, 0),
    (1, -1, 0),
    (1, 0, 1),
    (1, 0, -1),
    (0, 1, 1),
    (0, 1, -1),
)
BONDS = (
    ((0, 0, 0), (1, 0, 0)),
    ((0, 0, 0), (0, 1, 0)),
    ((0, 0, 0), (0, 0, 1)),
    ((0, 0, 0), (1, 1, 0)),
    ((1, 0, 0), (0, 1, 0)),
    ((0, 0, 0), (1, 0, 1)),
    ((1, 0, 0), (0, 0, 1)),
    ((0, 0, 0), (0, 1, 1)),
    ((0, 1, 0), (0, 0, 1)),
)
PAIRS = ((0, 0), (0, 1), (0, 2), (1, 1), (1, 2), (2, 2))
ENTRY = ((0, 1, 2), (1, 3, 4), (2, 4, 5))
time_step = 0.5
germanium_ratio = 1.5856
half_step = 0.5 * time_step
LEVELS = 2 * (STEPS + 1)
FIELDS = 9
GROUP = 4


def kernel(ring, half, *refs):
    blocks_in = refs[: 2 * ring]
    force_ref, table_ref, mass_grad, spring_grad = refs[2 * ring : 2 * ring + 4]
    (
        even_fields,
        odd_fields,
        speed,
        pushes,
        matter,
        inverse,
        coef,
        even_sums,
        odd_sums,
        even_carry,
        odd_carry,
        ray,
    ) = refs[2 * ring + 4 :]
    rows = 2 * half
    tiles = rows // TILE
    own_tiles = half // TILE
    me = lax.axis_index("gx")
    depth_index = lax.broadcasted_iota(jnp.int32, (TILE, ZCELLS), 1)

    def ahead(value):
        return pltpu.roll(value, ZCELLS - 1, 1)

    def behind(value):
        return pltpu.roll(value, 1, 1)

    def wrap(slab):
        return lax.rem(slab, ring)

    def at(tile, shift=0):
        return pl.ds(TILE * tile + shift, TILE)

    def late(tile, shift=0):
        return pl.ds(TILE + TILE * tile + shift, TILE)

    fields = (even_fields, odd_fields)
    sums_of = (even_sums, odd_sums)
    carry_of = (even_carry, odd_carry)

    def put_field(odd, number, slab, comp, tile, value):
        deeper = ahead(value)
        for place in (tile,) if tile else (0, tiles):
            fields[odd][0, number, slab, comp, at(place)] = value
            fields[odd][1, number, slab, comp, at(place)] = deeper

    for message in range(ring):
        slab = lax.bitwise_xor(me, message)
        for side in range(2):
            source = blocks_in[2 * message + side]
            for tile in range(own_tiles):
                target = side * own_tiles + tile
                for comp in range(3):
                    put_field(0, 0, slab, comp, target, source[comp, at(tile)])
                    rate = time_step * source[3 + comp, at(tile)]
                    speed[0, slab, comp, at(target)] = rate
                    speed[1, slab, comp, at(target)] = ahead(rate)
                sort = source[6, at(tile)]
                for which, value in ((0, sort), (1, source[8, at(tile)])):
                    deeper = ahead(value)
                    for place in (target,) if target else (0, tiles):
                        matter[which, 0, slab, at(place)] = value
                        matter[which, 1, slab, at(place)] = deeper
                mass = (1.0 + germanium_ratio * sort) * source[7, at(tile)]
                over_mass = (-time_step * time_step) / mass
                inverse[0, slab, at(target)] = over_mass
                inverse[1, slab, at(target)] = ahead(over_mass)

    def block_entries(direction):
        result = []
        for pair in range(3):
            index = table_ref[pair, direction]
            result.append([0.5 * (force_ref[index, a, b] + force_ref[index, b, a]) for a, b in PAIRS])
        return result

    inside = depth_index < ZCELLS - 1

    def matrix(entries, total_kind):
        low = total_kind < 0.5
        mixed = total_kind < 1.5
        return [
            jnp.where(low, entries[0][n], jnp.where(mixed, entries[1][n], entries[2][n])) for n in range(6)
        ]

    def ends(ref, where, slab, direction, tile):
        return [
            ref[where[0] + (dz,) + where[1] + (wrap(slab + dx),) + where[2] + (at(tile, dy),)]
            for dx, dy, dz in BONDS[direction]
        ]

    def matter_ends(which, slab, direction, tile):
        return ends(matter, ((which,), (), ()), slab, direction, tile)

    for direction in range(9):
        entries = block_entries(direction)

        def fill(pair, _, direction=direction, entries=entries):
            for slab, tile in [(GROUP * pair + which, tile) for which in range(GROUP) for tile in range(tiles)]:
                first, second = matter_ends(0, slab, direction, tile)
                spring_first, spring_second = matter_ends(1, slab, direction, tile)
                bond = 0.5 * (spring_first + spring_second)
                if BONDS[direction][1][2]:
                    bond = jnp.where(inside, bond, 0.0)
                for n, entry in enumerate(matrix(entries, first + second)):
                    coef[slab, 6 * direction + n, at(tile)] = bond * entry
            return 0

        lax.fori_loop(0, ring // GROUP, fill, 0)

    def product(entry, vector):
        return [
            entry[ENTRY[a][0]] * vector[0] + entry[ENTRY[a][1]] * vector[1] + entry[ENTRY[a][2]] * vector[2]
            for a in range(3)
        ]

    def bonds(odd, number, slab, order):
        beside = wrap(slab + 1)
        sums, carry = sums_of[odd], carry_of[odd]
        for tile in order:
            loaded = {}

            def site(place):
                if place not in loaded:
                    dx, dy, dz = place
                    loaded[place] = [
                        fields[odd][dz, number, beside if dx else slab, comp, at(tile, dy)] for comp in range(3)
                    ]
                return loaded[place]

            def force(direction):
                first, second = BONDS[direction]
                entry = [coef[slab, 6 * direction + n, at(tile)] for n in range(6)]
                return product(entry, [a - b for a, b in zip(site(first), site(second))])

            here, up, deep, across, lift, dive = (None,) * 6

            def add(total, values):
                return values if total is None else [a + b for a, b in zip(total, values)]

            def less(total, values):
                return [-b for b in values] if total is None else [a - b for a, b in zip(total, values)]

            f = force(0)
            here, across = f, f
            f = force(4)
            across, up = [a - b for a, b in zip(across, f)], f
            f = force(6)
            across, deep = [a - b for a, b in zip(across, f)], f
            f = force(1)
            here, up = add(here, f), add(up, f)
            f = force(2)
            here, deep = add(here, f), add(deep, f)
            f = force(8)
            up, deep = [a - b for a, b in zip(up, f)], add(deep, f)
            lift = force(3)
            here = add(here, lift)
            dive = force(5)
            here = add(here, dive)
            both = force(7)
            here = add(here, both)
            for comp in range(3):
                sums[0, slab, comp, late(tile)] = here[comp]
                sums[1, slab, comp, late(tile)] = up[comp]
                sums[2, slab, comp, late(tile)] = deep[comp]
                sums[3, slab, comp, late(tile)] = both[comp]
                carry[0, beside, comp, late(tile)] = across[comp]
                carry[1, beside, comp, late(tile)] = lift[comp]
                carry[2, beside, comp, late(tile)] = dive[comp]
                if tile == tiles - 1:
                    sums[1, slab, comp, late(-1)] = up[comp]
                    sums[3, slab, comp, late(-1)] = both[comp]
                    carry[1, beside, comp, late(-1)] = lift[comp]

    def update(odd, number, slab, order, kick, kind):
        mine = jnp.where(slab == me, 1, 0)
        sums, carry = sums_of[odd], carry_of[odd]
        detect = depth_index >= ZCELLS // 2
        detect = (detect, (depth_index >= ZCELLS // 2 - 1) & inside)
        for tile in order:
            over = [kick * inverse[frame, slab, at(tile)] for frame in range(2)]
            for comp in range(3):
                deep = sums[2, slab, comp, late(tile)] + carry[2, slab, comp, late(tile)]
                deep = deep + sums[3, slab, comp, late(tile, -1)]
                total = sums[0, slab, comp, late(tile)] - carry[0, slab, comp, late(tile)]
                total = total - (sums[1, slab, comp, late(tile, -1)] + carry[1, slab, comp, late(tile, -1)])
                for frame, force in enumerate((total - behind(deep), ahead(total) - deep)):
                    change = force * over[frame]
                    if kind != "dual" and frame == 0:
                        pushes[2 * number + odd, mine, comp, at(tile)] = change
                    moved = speed[frame, slab, comp, at(tile)] + change
                    if kind == "middle":
                        speed[frame, slab, comp, at(tile)] = jnp.zeros_like(moved)
                        fresh = jnp.where(detect[frame], moved, 0.0)
                    else:
                        speed[frame, slab, comp, at(tile)] = moved
                        fresh = fields[odd][frame, number, slab, comp, at(tile)] + moved
                    for place in (tile,) if tile else (0, tiles):
                        fields[1 - odd][frame, number + odd, slab, comp, at(place)] = fresh

    def span(level):
        count = jnp.minimum(ring, 2 * (LEVELS - level))
        low = jnp.where(count < ring, me + level + ring - LEVELS, me + 2 * level + ring // 2)
        return wrap(low + ring), count

    def middle_part(odd, number, order, kind, low, count, kick, below):
        def both(pair, _):
            for place in (2 * pair, 2 * pair + 1):
                for tile in below + order:
                    if tile in order:
                        update(odd, number, wrap(low + place + 1), [tile], kick, kind)
                    bonds(odd, number, wrap(low + place + 2), [tile])
            return 0

        lax.fori_loop(0, lax.div(count - 2, 2), both, 0)

    def step(odd, number, order, kind, final=False, below=()):
        level = 2 * number + odd
        low, count = span(level)
        kick = jnp.where((level == 0) | (level == STEPS) | (level == STEPS + 1), 0.5, 1.0)
        middle_part(odd, number, order, kind, low, count, kick, list(below))
        ahead_low = span(level + 1)[0]
        for place, slab in enumerate((wrap(low + count - 1), low)):
            for tile in order:
                if not final:
                    bonds(1 - odd, number + odd, wrap(ahead_low + place), [tile])
                update(odd, number, slab, [tile], kick, kind)

    everything = list(range(tiles))
    near = [tiles - 1] + list(range(own_tiles + 1))
    wide = LEVELS - TILE

    def run(start, stop, order, kind):
        level = start
        if level % 2:
            step(1, level // 2, order, kind)
            level += 1
        last = stop == LEVELS - 1
        pairs = (stop - level) // 2

        def two(number, _):
            step(0, number, order, kind)
            step(1, number, order, kind)
            return 0

        if pairs:
            lax.fori_loop(level // 2, level // 2 + pairs, two, 0)
        if (stop - level) % 2:
            step(0, stop // 2, order, kind, last)

    for place in range(2):
        bonds(0, 0, wrap(span(0)[0] + place), everything)
    run(0, wide - 1, everything, "state")
    step((wide - 1) % 2, (wide - 1) // 2, near, "state", below=[tiles - 2])
    run(wide, STEPS, near, "state")
    run(STEPS, STEPS + 1, near, "middle")
    run(STEPS + 1, LEVELS - 1, near, "dual")

    weights = [half_step if level in (0, STEPS) else time_step for level in range(STEPS + 1)]
    for tile in range(own_tiles):
        last = [fields[(STEPS + 1) % 2][0, (STEPS + 1) // 2, me, comp, at(tile)] for comp in range(3)]
        bar = 0.5 * (last[0] * last[0] + last[1] * last[1] + last[2] * last[2])
        for level in range(STEPS + 1):
            for comp in range(3):
                dual = fields[(LEVELS - 1 - level) % 2][0, (LEVELS - 1 - level) // 2, me, comp, at(tile)]
                bar = bar - dual * pushes[level, 1, comp, at(tile)]
        bar = bar * (1.0 / (time_step * time_step))
        mass_grad[at(tile)] = bar * (1.0 + germanium_ratio * matter[0, 0, me, at(tile)])

    entries_of = [block_entries(direction) for direction in range(9)]

    def strain(slab, direction, tile):
        first, second = matter_ends(0, slab, direction, tile)
        entry = matrix(entries_of[direction], first + second)
        result = None
        for level in range(STEPS + 1):
            parts = []
            for where in (level, LEVELS - 1 - level):
                pairs = [
                    ends(fields[where % 2], ((), (where // 2,), (comp,)), slab, direction, tile)
                    for comp in range(3)
                ]
                parts.append([a - b for a, b in pairs])
            state, dual = parts
            image = product(entry, dual)
            term = state[0] * image[0] + state[1] * image[1] + state[2] * image[2]
            term = weights[level] / time_step * term
            result = term if result is None else result + term
        if BONDS[direction][1][2]:
            result = jnp.where(inside, result, 0.0)
        return result

    past = wrap(me + ring - 1)

    def lifted(tile):
        up = strain(me, 1, tile) + strain(me, 4, tile) + strain(me, 8, tile) + strain(past, 3, tile)
        return up, strain(me, 7, tile)

    def rays(tile, _):
        second = strain(me, 1, tile)
        both = strain(me, 7, tile)
        third = strain(me, 2, tile)
        here = strain(me, 0, tile) + second + third + strain(me, 3, tile) + strain(me, 5, tile) + both
        here = here + strain(past, 0, tile) + strain(past, 4, tile) + strain(past, 6, tile)
        eighth = strain(me, 8, tile)
        ray[0, late(tile)] = here
        ray[1, late(tile)] = second + strain(me, 4, tile) + eighth + strain(past, 3, tile)
        ray[2, late(tile)] = third + strain(me, 6, tile) + eighth + strain(past, 5, tile)
        ray[3, late(tile)] = both
        return 0

    lax.fori_loop(0, own_tiles, rays, 0)
    ray[1, late(-1)], ray[3, late(-1)] = lifted(tiles - 1)
    for tile in range(own_tiles):
        deep = ray[2, late(tile)] + ray[3, late(tile, -1)]
        spring_grad[at(tile)] = -0.5 * (ray[0, late(tile)] + ray[1, late(tile, -1)] + behind(deep))


def pack(displacement, velocity, species, mass_factor, spring, packed):
    for comp in range(3):
        packed[comp] = displacement[comp, 0]
        packed[3 + comp] = velocity[comp, 0]
    packed[6] = species[0].astype(jnp.float32)
    packed[7] = mass_factor[0]
    packed[8] = spring[0]


def gathered_body(displacement, velocity, species, mass_factor, spring, force_blocks, shell_table):
    ring = lax.axis_size("gx")
    half = spring.shape[1]
    rows = 2 * half
    own = pl.pallas_call(
        pack,
        out_shape=jax.ShapeDtypeStruct((FIELDS, half, ZCELLS), jnp.float32),
        in_specs=[pl.BlockSpec(memory_space=pltpu.VMEM)] * 5,
        out_specs=pl.BlockSpec(memory_space=pltpu.VMEM),
    )(displacement, velocity, species, mass_factor, spring)

    def swap_slabs(value, mask):
        return lax.ppermute(value, "gx", [(i, i ^ mask) for i in range(ring)])

    def swap_halves(value):
        return lax.ppermute(value, "gy", [(0, 1), (1, 0)])

    messages = {0: own, 1: swap_slabs(own, 1)}
    for mask in range(2, ring, 2):
        messages[mask] = swap_slabs(own, mask)
        messages[mask + 1] = swap_slabs(messages[mask], 1)
    operands = []
    for mask in range(ring):
        operands += [messages[mask], swap_halves(messages[mask])]

    padded = rows + TILE
    scratch = [
        (2, LEVELS // 2, ring, 3, padded, ZCELLS),
        (2, LEVELS // 2, ring, 3, padded, ZCELLS),
        (2, ring, 3, rows, ZCELLS),
        (STEPS + 1, 2, 3, rows, ZCELLS),
        (2, 2, ring, padded, ZCELLS),
        (2, ring, rows, ZCELLS),
        (ring, 54, rows, ZCELLS),
        (4, ring, 3, padded, ZCELLS),
        (4, ring, 3, padded, ZCELLS),
        (3, ring, 3, padded, ZCELLS),
        (3, ring, 3, padded, ZCELLS),
        (4, padded, ZCELLS),
    ]
    mass_grad, spring_grad = pl.pallas_call(
        lambda *refs: kernel(ring, half, *refs),
        out_shape=[jax.ShapeDtypeStruct((half, ZCELLS), jnp.float32)] * 2,
        in_specs=[pl.BlockSpec(memory_space=pltpu.VMEM)] * (2 * ring)
        + [pl.BlockSpec(memory_space=pltpu.SMEM)] * 2,
        out_specs=[pl.BlockSpec(memory_space=pltpu.VMEM)] * 2,
        scratch_shapes=[pltpu.VMEM(shape, jnp.float32) for shape in scratch],
        compiler_params=pltpu.CompilerParams(vmem_limit_bytes=60 * 1024 * 1024),
    )(*operands, force_blocks, shell_table)
    return mass_grad[None], spring_grad[None]


def padded_2(cells, sides, width):
    for axis, dim in sides:
        count = lax.axis_size(axis)
        head = lax.slice_in_dim(cells, 0, width, axis=dim)
        tail = lax.slice_in_dim(cells, cells.shape[dim] - width, cells.shape[dim], axis=dim)
        cells = jnp.concatenate(
            [
                lax.ppermute(tail, axis, [(i, (i + 1) % count) for i in range(count)]),
                cells,
                lax.ppermute(head, axis, [((i + 1) % count, i) for i in range(count)]),
            ],
            axis=dim,
        )
    return cells


def shift_depth(field, depth):
    if depth == 0:
        return field
    border = jnp.zeros_like(field[..., :1])
    if depth > 0:
        return jnp.concatenate([field[..., 1:], border], axis=-1)
    return jnp.concatenate([border, field[..., :-1]], axis=-1)


def pair_blocks(force_blocks, shell_table):
    symmetric = 0.5 * (force_blocks + jnp.swapaxes(force_blocks, 1, 2))
    labels = jnp.arange(force_blocks.shape[0], dtype=jnp.int32)
    selector = (shell_table[:, :, None] == labels[None, None, :]).astype(jnp.float32)
    return jnp.einsum("kdn,nrc->kdrc", selector, symmetric, precision=lax.Precision.HIGHEST)


def coupling(kinds, centre_kind, other_kind, valid):
    weight_low = (1.0 - centre_kind) * (1.0 - other_kind)
    weight_high = centre_kind * other_kind
    weight_mixed = 1.0 - weight_low - weight_high
    return [
        [
            (
                weight_low * kinds[0, first, second]
                + weight_mixed * kinds[1, first, second]
                + weight_high * kinds[2, first, second]
            )
            * valid
            for second in range(3)
        ]
        for first in range(3)
    ]


def apply_coupling(matrix, difference):
    return jnp.stack(
        [
            matrix[first][0] * difference[0]
            + matrix[first][1] * difference[1]
            + matrix[first][2] * difference[2]
            for first in range(3)
        ]
    )


def operator_terms(
    value, value_at, partner, partner_at, species_float, spring, params_at, valid_at, blocks
):
    total = jnp.zeros_like(value)
    spring_part = jnp.zeros_like(spring)
    for direction in range(9):
        for flipped in (1, -1):
            offset = tuple((flipped * entry for entry in DIRECTIONS[direction]))
            other_kind, other_spring = params_at(offset)
            matrix = coupling(blocks[:, direction], species_float, other_kind, valid_at(offset))
            image = apply_coupling(matrix, value - value_at(offset))
            total = total + 0.5 * (spring + other_spring) * image
            if partner is not None:
                spring_part = spring_part + 0.5 * jnp.sum(
                    (partner - partner_at(offset)) * image, axis=0
                )
    return (total, spring_part)


def pick(padded, offset):
    width_x = padded.shape[1] - 2
    width_y = padded.shape[2] - 2
    window = padded[
        :, 1 + offset[0] : 1 + offset[0] + width_x, 1 + offset[1] : 1 + offset[1] + width_y, :
    ]
    return shift_depth(window, offset[2])


def centre(padded):
    return padded[:, 1:-1, 1:-1, :]


def pad_state(field):
    return padded_2(field, (("gx", 1), ("gy", 2)), 1)


def exchanged_body(displacement, velocity, species, mass_factor, spring, force_blocks, shell_table):
    blocks = pair_blocks(force_blocks, shell_table)
    species_float = species.astype(jnp.float32)
    species_mass = 1.0 + germanium_ratio * species_float
    mass = species_mass * mass_factor
    material = padded_2(jnp.stack([species_float, spring]), (("gx", 1), ("gy", 2)), 1)
    filled = jnp.ones_like(spring)

    def params_at(offset):
        beside_all = pick(material, offset)
        return (beside_all[0], beside_all[1])

    def valid_at(offset):
        return shift_depth(filled, offset[2])

    def acting(padded_value, padded_partner):
        value_at = lambda offset: pick(padded_value, offset)
        if padded_partner is None:
            return operator_terms(
                centre(padded_value),
                value_at,
                None,
                None,
                species_float,
                spring,
                params_at,
                valid_at,
                blocks,
            )
        partner_at = lambda offset: pick(padded_partner, offset)
        return operator_terms(
            centre(padded_value),
            value_at,
            centre(padded_partner),
            partner_at,
            species_float,
            spring,
            params_at,
            valid_at,
            blocks,
        )

    half_step = 0.5 * time_step
    drift = 0.5 * time_step * time_step
    states = [displacement]
    padded_states = [pad_state(displacement)]
    accels = [-acting(padded_states[0], None)[0] / mass]
    moving = velocity
    for count in range(STEPS):
        advanced = states[-1] + time_step * moving + drift * accels[-1]
        padded_advanced = pad_state(advanced)
        fresh = -acting(padded_advanced, None)[0] / mass
        moving = moving + half_step * (accels[-1] + fresh)
        states.append(advanced)
        padded_states.append(padded_advanced)
        accels.append(fresh)
    depth_index = lax.broadcasted_iota(jnp.int32, spring.shape, 2)
    detect = (depth_index >= ZCELLS // 2).astype(jnp.float32)
    velocity_bar = detect * mass * moving
    mass_bar = 0.5 * detect * jnp.sum(moving * moving, axis=0)
    spring_bar = jnp.zeros_like(spring)
    state_bar = jnp.zeros_like(displacement)
    accel_bar = jnp.zeros_like(displacement)
    for level in range(STEPS, -1, -1):
        if level > 0:
            accel_bar = accel_bar + half_step * velocity_bar
        scaled = accel_bar / mass
        padded_scaled = padded_2(scaled, (("gx", 1), ("gy", 2)), 1)
        padded_partner = padded_states[level]
        pushed, spring_term = acting(padded_scaled, padded_partner)
        state_bar = state_bar - pushed
        mass_bar = mass_bar - jnp.sum(accel_bar * accels[level], axis=0) / mass
        spring_bar = spring_bar - spring_term
        if level > 0:
            accel_bar = drift * state_bar + half_step * velocity_bar
            velocity_bar = velocity_bar + time_step * state_bar
    return (mass_bar * species_mass, spring_bar)


def solution(mesh):
    small = mesh.shape["gx"] == 8 and mesh.shape["gy"] == 2
    return jax.shard_map(
        gathered_body if small else exchanged_body,
        mesh=mesh,
        in_specs=(
            P(None, ("groups", "gx"), "gy", None),
            P(None, ("groups", "gx"), "gy", None),
            P("gx", "gy", None),
            P("gx", "gy", None),
            P("gx", "gy", None),
            P(),
            P(),
        ),
        out_specs=(P(("groups", "gx"), "gy", None), P(("groups", "gx"), "gy", None)),
        check_vma=False,
    )
```
